128 devices in a mesh: row: 8 (over y, z_hi), col: 16 (over z_lo, x, core).
Axes of the slice: x: 4, y: 4, z: 4 (z_hi: 2, z_lo: 2; z = z_hi * 2 + z_lo), core: 2. Of those that a mesh axis runs over, the one named last changes fastest.
Arguments:
- counts: int32 [256, 32768], P('col', 'row'), may hold values from 0 to 1591, as said below
- whiten: bfloat16 [64, 512, 512], P('row'), may hold values from -0.75 to 0.75
- initial_tiles: float32 [8, 16, 96, 128, 128], P('row', 'col'), as said below
- tile_rows: int32 [8, 16, 96], P('row', 'col'), may hold values from 0 to 31, as said below
- tile_cols: int32 [8, 16, 96], P('row', 'col'), may hold values from 0 to 15
- tile_count: int32 [8, 16], P('row', 'col'), may hold values from 16 to 96, as said below
Outputs:
- precision: float32 [8, 16, 96, 128, 128], P('row', 'col')
- last_grad: float32 [8, 16, 96, 128, 128], P('row', 'col')
The draws below stay inside these ranges and needn't reach their ends.
Inputs may be any that keep to these rules, and one draw needn't show every extreme that they name: Nonnegative k-mer counts. `tile_rows`: with tile_cols, the slots of one device name distinct tiles of its 32 x 16 grid; every tile on the global diagonal is named by a live slot. `tile_count`: some device has 96 live slots. `initial_tiles`: diagonal entries of diagonal tiles lie between 0.5 and 2.
All inputs are finite; a program needn't handle non-finite values.
Results may differ from the reference program's by a relative error of at most 0.025.
Values may be sent and summed in bfloat16 or wider, within the bound.
A program may use at most 192 MiB of HBM per device.

```python
import jax
import jax.numpy as jnp
from jax import lax

TILE = 128
TILE_ROWS = 32
TILE_COLS = 16
ROW_GROUPS = 8
COL_GROUPS = 16
FEATURES = 32768
BLOCK = 512
SAMPLES = 256
SLOTS = 96
ITERS = 2


def tile_pattern(key):
    base = jax.random.fold_in(key, 11)
    cells = TILE_ROWS * TILE_COLS
    cell = jnp.arange(cells, dtype=jnp.int32)
    group_r = jnp.arange(ROW_GROUPS, dtype=jnp.int32)[:, None, None]
    group_c = jnp.arange(COL_GROUPS, dtype=jnp.int32)[None, :, None]
    diagonal = group_r * TILE_ROWS + cell // TILE_COLS == group_c * TILE_COLS + cell % TILE_COLS
    noise = jax.random.randint(base, (ROW_GROUPS, COL_GROUPS, cells), 0, 1 << 20, dtype=jnp.int32)
    score = jnp.where(diagonal, cell - cells, noise * cells + cell)
    picked = lax.top_k(-score, SLOTS)[1].astype(jnp.int32)
    return (picked // TILE_COLS, picked % TILE_COLS)


def draw_tile_rows(key, part):
    return tile_pattern(key)[0]


def draw_tile_cols(key, part):
    return tile_pattern(key)[1]


def draw_tile_count(key, part):
    first = jax.random.fold_in(key, 21)
    second = jax.random.fold_in(key, 22)
    loads = jax.random.randint(first, (ROW_GROUPS, COL_GROUPS), SLOTS // 6, SLOTS * 2 // 3 + 1, dtype=jnp.int32)
    loads = jnp.maximum(loads, TILE_COLS)
    busiest = jax.random.randint(second, (), 0, ROW_GROUPS * COL_GROUPS, dtype=jnp.int32)
    flat = loads.reshape(-1).at[busiest].set(SLOTS)
    return flat.reshape(ROW_GROUPS, COL_GROUPS).astype(jnp.int32)


def draw_initial_tiles(key, part):
    slot_rows, slot_cols = tile_pattern(key)
    group_r = jnp.arange(ROW_GROUPS, dtype=jnp.int32)[:, None, None]
    group_c = jnp.arange(COL_GROUPS, dtype=jnp.int32)[None, :, None]
    tile_diag = group_r * TILE_ROWS + slot_rows == group_c * TILE_COLS + slot_cols
    first = jax.random.fold_in(key, 31)
    second = jax.random.fold_in(key, 32)
    shape = (ROW_GROUPS, COL_GROUPS, SLOTS, TILE, TILE)
    spread = 0.1 * jax.random.normal(first, shape, jnp.float32)
    leading = jax.random.uniform(second, shape[:-1], jnp.float32, 0.8, 1.6)
    identity = jnp.arange(TILE)[:, None] == jnp.arange(TILE)[None, :]
    on_diag = tile_diag[:, :, :, None, None] & identity
    return jnp.where(on_diag, leading[..., None], spread).astype(jnp.float32)


def draw_counts(key, part):
    sample = jnp.arange(SAMPLES, dtype=jnp.int32)[:, None]
    feature = jnp.arange(FEATURES, dtype=jnp.int32)[None, :]
    factor = jax.random.randint(jax.random.fold_in(key, 41), (1, FEATURES), 1, 17, dtype=jnp.int32)
    drawn = jax.random.randint(jax.random.fold_in(key, 42), (SAMPLES, FEATURES), 0, 99 * factor, dtype=jnp.int32)
    corner = (sample == SAMPLES - 1) & (feature == 0)
    return jnp.where(corner, jnp.int32(1591), drawn).astype(jnp.int32)


def steps_of(key, shape, shards, smallest, top_value):
    def one(axis_at, blocks):
        heights = jax.random.uniform(jax.random.fold_in(jax.random.fold_in(key, 6), axis_at), (blocks,), jnp.float32, smallest / len(shards), top_value / len(shards))
        return jnp.repeat(jnp.exp(heights), shape[axis_at] // blocks).reshape((-1,) + (1,) * (len(shape) - axis_at - 1))

    gain = one(*shards[0])
    for cut in shards[1:]:
        gain = gain * one(*cut)
    return gain


def gaussian(rng, dims, width, most, pieces=(), kind=jnp.bfloat16):
    level = steps_of(rng, dims, pieces, -0.22, 0.18) if pieces else 1.0
    values = jax.random.normal(rng, dims, jnp.float32) * width * level
    return jnp.minimum(jnp.maximum(values, -most), most).astype(kind)


def setup_inputs(seed: int = 0) -> dict:
    keys = jax.random.split(jax.random.key(seed), 7)
    counts = draw_counts(jax.random.fold_in(keys[6], 71), 0)
    whiten = gaussian(keys[1], (FEATURES // BLOCK, BLOCK, BLOCK), (BLOCK // 8) ** -0.5, 0.75, ((0, 8),))
    initial_tiles = draw_initial_tiles(jax.random.fold_in(keys[6], 71), 0)
    tile_rows = draw_tile_rows(jax.random.fold_in(keys[6], 71), 0)
    tile_cols = draw_tile_cols(jax.random.fold_in(keys[6], 71), 0)
    tile_count = draw_tile_count(jax.random.fold_in(keys[6], 71), 0)
    return dict(counts=counts, whiten=whiten, initial_tiles=initial_tiles, tile_rows=tile_rows, tile_cols=tile_cols, tile_count=tile_count)


step_size = 0.08
penalty = 1.0
epsilon = 1e-05

def rows_partial(omega_low, slot_rows, slot_cols, column_x):
    picked = jnp.take(column_x, slot_cols, axis=1).astype(jnp.float32)
    slot_terms = jnp.einsum('kaq,nkq->kan', omega_low.astype(jnp.float32), picked, precision=lax.Precision.HIGHEST)
    row_hot = (slot_rows[None, :] == jnp.arange(TILE_ROWS, dtype=jnp.int32)[:, None]).astype(jnp.float32)
    return jnp.einsum('tk,kan->tan', row_hot, slot_terms, precision=lax.Precision.HIGHEST)

def cols_partial(omega_low, slot_rows, slot_cols, row_x):
    picked = jnp.take(row_x, slot_rows, axis=1).astype(jnp.float32)
    slot_terms = jnp.einsum('nka,kaq->knq', picked, omega_low.astype(jnp.float32), precision=lax.Precision.HIGHEST)
    col_hot = (slot_cols[None, :] == jnp.arange(TILE_COLS, dtype=jnp.int32)[:, None]).astype(jnp.float32)
    return jnp.einsum('sk,knq->nsq', col_hot, slot_terms, precision=lax.Precision.HIGHEST)

def rounded(value):
    return lax.optimization_barrier(value.astype(jnp.bfloat16)).astype(jnp.float32)

def reference(counts, whiten, initial_tiles, tile_rows, tile_cols, tile_count):
    logged = jnp.log1p(counts.astype(jnp.float32))
    feature_mean = lax.optimization_barrier(jnp.mean(logged, axis=0))
    centered = logged - feature_mean
    variance = lax.optimization_barrier(jnp.mean(centered * centered, axis=0))
    standard = (centered * lax.rsqrt(variance + epsilon)).astype(jnp.bfloat16)
    blocks = standard.reshape(SAMPLES, FEATURES // BLOCK, BLOCK).astype(jnp.float32)
    whitened = jnp.einsum('nbw,bwv->nbv', blocks, whiten.astype(jnp.float32), precision=lax.Precision.HIGHEST)
    whitened = whitened.astype(jnp.bfloat16).reshape(SAMPLES, FEATURES)
    row_x = whitened.reshape(SAMPLES, ROW_GROUPS, TILE_ROWS, TILE)
    column_x = whitened.reshape(SAMPLES, COL_GROUPS, TILE_COLS, TILE)
    live_slots = (jnp.arange(SLOTS, dtype=jnp.int32)[None, None, :] < tile_count[:, :, None]).astype(jnp.float32)
    omega = initial_tiles * live_slots[:, :, :, None, None]
    identity = jnp.arange(TILE)[:, None] == jnp.arange(TILE)[None, :]
    gradient = jnp.zeros_like(omega)
    for iteration in range(ITERS):
        omega_low = omega.astype(jnp.bfloat16)

        def row_block(group_r):

            def add(carry, group_c):
                part = rows_partial(omega_low[group_r, group_c], tile_rows[group_r, group_c], tile_cols[group_r, group_c], column_x[:, group_c])
                return (carry + rounded(part), None)
            start = jnp.zeros((TILE_ROWS, TILE, SAMPLES), jnp.float32)
            return lax.scan(add, start, jnp.arange(COL_GROUPS, dtype=jnp.int32))[0]

        def column_block(group_c):

            def add(carry, group_r):
                part = cols_partial(omega_low[group_r, group_c], tile_rows[group_r, group_c], tile_cols[group_r, group_c], row_x[:, group_r])
                return (carry + rounded(part), None)
            start = jnp.zeros((SAMPLES, TILE_COLS, TILE), jnp.float32)
            return lax.scan(add, start, jnp.arange(ROW_GROUPS, dtype=jnp.int32))[0]
        row_terms = lax.map(row_block, jnp.arange(ROW_GROUPS, dtype=jnp.int32)).astype(jnp.bfloat16)
        column_terms = lax.map(column_block, jnp.arange(COL_GROUPS, dtype=jnp.int32)).astype(jnp.bfloat16)

        def update(device):
            group_r = device // COL_GROUPS
            group_c = device % COL_GROUPS
            slot_rows = tile_rows[group_r, group_c]
            slot_cols = tile_cols[group_r, group_c]
            u_pick = jnp.take(row_terms[group_r], slot_rows, axis=0).astype(jnp.float32)
            xc_pick = jnp.take(column_x[:, group_c], slot_cols, axis=1).astype(jnp.float32)
            xr_pick = jnp.take(row_x[:, group_r], slot_rows, axis=1).astype(jnp.float32)
            v_pick = jnp.take(column_terms[group_c], slot_cols, axis=1).astype(jnp.float32)
            left = jnp.einsum('kan,nkq->kaq', u_pick, xc_pick, precision=lax.Precision.HIGHEST)
            right = jnp.einsum('nka,nkq->kaq', xr_pick, v_pick, precision=lax.Precision.HIGHEST)
            live_here = live_slots[group_r, group_c][:, None, None]
            grad = 0.5 * (left + right) / SAMPLES * live_here
            current = omega[group_r, group_c]
            moved = current - step_size * grad
            shrunk = jnp.sign(moved) * jnp.maximum(jnp.abs(moved) - step_size * penalty, 0.0)
            diagonal = 0.5 * (moved + jnp.sqrt(moved * moved + 4.0 * step_size))
            tile_diag = group_r * TILE_ROWS + slot_rows == group_c * TILE_COLS + slot_cols
            on_diag = tile_diag[:, None, None] & identity[None, :, :]
            fresh = jnp.where(on_diag, diagonal, shrunk) * live_here
            return (fresh, grad)
        fresh, grads = lax.map(update, jnp.arange(ROW_GROUPS * COL_GROUPS, dtype=jnp.int32))
        omega = fresh.reshape(ROW_GROUPS, COL_GROUPS, SLOTS, TILE, TILE)
        gradient = grads.reshape(ROW_GROUPS, COL_GROUPS, SLOTS, TILE, TILE)
    return (omega, gradient)
```

```python
import functools

import jax
import jax.numpy as jnp
from jax import lax
from jax.experimental import pallas as pl
from jax.experimental.pallas import tpu as pltpu
from jax.sharding import PartitionSpec as P

step_size = 0.08
penalty = 1.0
epsilon = 1e-05
MESH = pl.DeviceIdType.MESH
F32 = jnp.float32
BF16 = jnp.bfloat16
GROUP = 8
LIMIT = 40 * 2**20


class Place:
    def __init__(self):
        self.row = lax.axis_index("row")
        self.col = lax.axis_index("col")
        self.y, self.zh = self.row // 2, self.row % 2
        self.zl, self.x, self.core = self.col // 8, (self.col // 2) % 4, self.col % 2
        self.mine = self.core * 8 + self.x * 2 + self.zl
        self.mine_col = self.row

    def at(self, row=None, col=None):
        return (self.row if row is None else row, self.col if col is None else col)

    def xpeer(self, d):
        return self.at(col=self.zl * 8 + ((self.x + d) % 4) * 2 + self.core)

    def ypeer(self, d):
        return self.at(row=((self.y + d) % 4) * 2 + self.zh)

    def zlpeer(self):
        return self.at(col=(1 - self.zl) * 8 + self.x * 2 + self.core)

    def zhpeer(self):
        return self.at(row=self.y * 2 + 1 - self.zh)

    def sibling(self):
        return self.at(col=self.zl * 8 + self.x * 2 + 1 - self.core)


class Wire:
    def __init__(self, send_sem, recv_sem):
        self.send_sem, self.recv_sem = send_sem, recv_sem
        self.copies = {}

    def send(self, name, src, dst, device):
        i = len(self.copies)
        copy = pltpu.make_async_remote_copy(
            src_ref=src, dst_ref=dst, send_sem=self.send_sem.at[i],
            recv_sem=self.recv_sem.at[i], device_id=device, device_id_type=MESH,
        )
        copy.start()
        self.copies[name] = copy

    def recv(self, *names):
        for name in names:
            self.copies[name].wait_recv()

    def drain(self):
        for copy in self.copies.values():
            copy.wait_send()


class Gather:
    def __init__(self, wire, tag, out, base, position, z, ring, zpeer, sibling, done):
        self.w, self.tag, self.out = wire, tag, out
        self.base, self.position, self.z = base, position, z
        self.ring, self.zpeer, self.sibling, self.done = ring, zpeer, sibling, done

    def slot(self, d, other):
        z = 1 - self.z if other else self.z
        return self.base + ((self.position + d) % 4) * 2 + z

    def pass_on(self, name, slot, device):
        self.w.send(self.tag + name, self.out.at[slot], self.out.at[slot], device)

    def have(self, name, slot):
        if self.sibling is not None:
            self.pass_on("core" + name, slot, self.sibling)

    def own(self):
        s = self.slot(0, False)
        self.pass_on("z", s, self.zpeer)
        self.pass_on("own+", s, self.ring(1))
        self.pass_on("own-", s, self.ring(3))
        self.have("own", s)
        self.done(s)

    def other(self):
        s = self.slot(0, True)
        self.w.recv(self.tag + "z")
        self.pass_on("other+", s, self.ring(1))
        self.pass_on("other-", s, self.ring(3))
        self.have("other", s)
        self.done(s)

    def relay(self):
        left, right = self.slot(3, False), self.slot(1, True)
        self.w.recv(self.tag + "own+")
        self.pass_on("far+", left, self.ring(1))
        self.have("a", left)
        self.w.recv(self.tag + "other-")
        self.pass_on("far-", right, self.ring(3))
        self.have("b", right)
        self.done(left)
        self.done(right)

    def near(self):
        left, right = self.slot(3, True), self.slot(1, False)
        self.w.recv(self.tag + "own-")
        self.have("c", right)
        self.w.recv(self.tag + "other+")
        self.have("d", left)
        self.done(right)
        self.done(left)

    def far(self):
        a, b = self.slot(2, False), self.slot(2, True)
        self.w.recv(self.tag + "far+")
        self.have("e", a)
        self.w.recv(self.tag + "far-")
        self.have("f", b)
        self.done(a)
        self.done(b)

    def rest(self):
        if self.sibling is None:
            return
        flip = 8 - 2 * self.base
        for name, d, other in (
            ("own", 0, 0), ("other", 0, 1), ("a", 3, 0), ("b", 1, 1),
            ("c", 1, 0), ("d", 3, 1), ("e", 2, 0), ("f", 2, 1),
        ):
            self.w.recv(self.tag + "core" + name)
            self.done(self.slot(d, other) + flip)


def row_gather(wire, place, out, done):
    return Gather(wire, "r", out, place.core * 8, place.x, place.zl, place.xpeer, place.zlpeer(), place.sibling(), done)


def col_gather(wire, place, out, done):
    return Gather(wire, "c", out, 0, place.y, place.zh, place.ypeer, place.zhpeer(), None, done)


def greet(devices):
    barrier = pltpu.get_barrier_semaphore()
    for device in devices:
        pl.semaphore_signal(barrier, inc=1, device_id=device, device_id_type=MESH)
    return barrier


def prep_kernel(counts, whiten, xr, xc, xrt, xct, packed, landed, wbuf, wsem, lsem, send_sem, recv_sem):
    place = Place()
    block, half = place.mine // 2, place.mine % 2
    to_row, to_col = place.x * 2 + place.zl, 2 * place.row + place.core
    from_row, from_col = place.col // 2, (place.row % 2) * 8 + (place.row // 2) * 2 + place.core
    moves = jnp.logical_or(to_row != place.row, to_col != place.col)
    peers = [place.at(col=(place.col + d) % 16) for d in range(1, 16)]
    peers += [place.ypeer(d) for d in (1, 3)] + [place.zhpeer()]
    barrier = greet(peers)

    @pl.when(moves)
    def _():
        for device in ((to_row, to_col), (from_row, from_col)):
            pl.semaphore_signal(barrier, inc=1, device_id=device, device_id_type=MESH)

    load = pltpu.make_async_copy(
        whiten.at[block, :, pl.ds(pl.multiple_of(half * 256, 256), 256)], wbuf, wsem
    )
    load.start()
    for b in range(8):
        packed[b] = counts[:, b * 512 : (b + 1) * 512].astype(jnp.int16)
    pl.semaphore_wait(barrier, len(peers) + 2 * moves.astype(jnp.int32))

    wire = Wire(send_sem, recv_sem)
    for d in range(1, 16):
        c = (place.col + d) % 16
        b = (c % 2) * 4 + (c // 2) % 4
        wire.send(f"a{d}", packed.at[b], landed.at[place.col], place.at(col=c))
    landed[place.col] = packed[block]
    wire.recv(*[f"a{d}" for d in range(1, 16)])
    load.wait()
    logged = jnp.log(1.0 + landed[...].astype(jnp.int32).astype(F32)).reshape(256, 512)
    mean = jnp.mean(logged, axis=0, keepdims=True)
    centered = logged - mean
    variance = jnp.mean(centered * centered, axis=0, keepdims=True)
    standard = (centered * lax.rsqrt(variance + epsilon)).astype(BF16)
    whitened = jnp.dot(standard, wbuf[...], preferred_element_type=F32).astype(BF16)
    xr[place.mine, :256] = whitened[:, :128]
    xr[place.mine, 256:] = whitened[:, 128:]

    def turn(source, target):
        def done(s):
            target[s, :128] = source[s, :256].T
            target[s, 128:] = source[s, 256:].T

        return done

    row = row_gather(wire, place, xr, turn(xr, xrt))
    col = col_gather(wire, place, xc, turn(xc, xct))
    hop = pltpu.make_async_remote_copy(
        src_ref=xr.at[place.mine], dst_ref=xc.at[to_row], send_sem=lsem.at[0],
        recv_sem=lsem.at[1], device_id=(to_row, to_col), device_id_type=MESH,
    )

    @pl.when(moves)
    def _():
        hop.start()

    @pl.when(jnp.logical_not(moves))
    def _():
        xc[place.mine_col] = xr[place.mine]

    row.own()

    @pl.when(moves)
    def _():
        hop.wait_recv()

    col.own()
    row.other()
    col.other()
    row.relay()
    col.relay()
    row.near()
    col.near()
    row.far()
    col.far()
    row.rest()
    wire.drain()

    @pl.when(moves)
    def _():
        hop.wait_send()


def add(*parts):
    total = parts[0].astype(F32)
    for part in parts[1:]:
        total = total + part.astype(F32)
    return total


class Scatter:
    def __init__(self, wire, tag, land, zland, keep, zout, z, ring, zpeer, pick, stage):
        self.w, self.tag, self.land, self.zland = wire, tag, land, zland
        self.keep, self.zout, self.z = keep, zout, z
        self.ring, self.zpeer, self.pick, self.stage = ring, zpeer, pick, stage

    def put(self, name, i, src, device):
        self.w.send(self.tag + name, src, self.land.at[i], device)

    def first(self):
        self.put("A1", 0, self.stage(2, 0), self.ring(1))
        self.put("B1", 1, self.stage(2, 1), self.ring(3))

    def second(self):
        self.put("A2", 2, self.stage(1, 1), self.ring(1))
        self.put("B2", 3, self.stage(3, 0), self.ring(3))

    def merge(self):
        self.w.recv(self.tag + "A1")
        self.land[0] = add(self.pick(1, 0), self.land[0]).astype(BF16)
        self.put("A3", 4, self.land.at[0], self.ring(1))
        self.w.recv(self.tag + "B1")
        self.land[1] = add(self.pick(3, 1), self.land[1]).astype(BF16)
        self.put("B3", 5, self.land.at[1], self.ring(3))

    def cross(self):
        self.w.recv(*[self.tag + n for n in ("B2", "A2", "A3", "B3")])
        own = (add(self.pick(0, 0), self.land[3], self.land[4]), add(self.pick(0, 1), self.land[2], self.land[5]))
        mine = self.z == 0
        self.zout[...] = jnp.where(mine, own[1], own[0]).astype(BF16)
        self.w.send(self.tag + "Z", self.zout, self.zland, self.zpeer)
        self.keep[...] = jnp.where(mine, own[0], own[1])

    def last(self, out, slot):
        self.w.recv(self.tag + "Z")
        out[slot] = add(self.keep[...], self.zland[...]).astype(BF16)


def reduce_kernel(
    rp, cp, u, v, pair, summed, rland, rzland, rkeep, rzout, cland, czland, ckeep, czout, send_sem, recv_sem
):
    place = Place()
    peers = [place.sibling(), place.xpeer(1), place.xpeer(3), place.zlpeer()]
    peers += [place.ypeer(1), place.ypeer(3), place.zhpeer()]
    barrier = greet(peers)
    pl.semaphore_wait(barrier, len(peers))
    wire = Wire(send_sem, recv_sem)
    here, there = place.core * 8, 8 - place.core * 8

    def rslot(d, e):
        return ((place.x + d) % 4) * 2 + e

    def cslot(d, e):
        return ((place.y + d) % 4) * 2 + e

    order = ((2, 0), (2, 1), (1, 1), (3, 0), (1, 0), (3, 1), (0, 0), (0, 1))
    for d, e in order:
        s = rslot(d, e)
        wire.send(f"s{d}{e}", rp.at[there + s], pair.at[s], place.sibling())
    col = Scatter(
        wire, "cs", cland, czland, ckeep, czout, place.zh, place.ypeer, place.zhpeer(),
        lambda d, e: cp[cslot(d, e)], lambda d, e: cp.at[cslot(d, e)],
    )
    row = Scatter(
        wire, "rs", rland, rzland, rkeep, rzout, place.zl, place.xpeer, place.zlpeer(),
        lambda d, e: summed[rslot(d, e)], lambda d, e: summed.at[rslot(d, e)],
    )
    col.first()
    col.second()

    def join(d, e):
        s = rslot(d, e)
        wire.recv(f"s{d}{e}")
        summed[s] = add(rp[here + s], pair[s]).astype(BF16)

    for d, e in order[:2]:
        join(d, e)
    row.first()
    for d, e in order[2:4]:
        join(d, e)
    row.second()
    for d, e in order[4:]:
        join(d, e)
    col.merge()
    row.merge()
    col.cross()
    row.cross()
    nothing = lambda s: None
    rg = row_gather(wire, place, u, nothing)
    cg = col_gather(wire, place, v, nothing)
    col.last(v, place.mine_col)
    cg.own()
    row.last(u, place.mine)
    rg.own()
    cg.other()
    rg.other()
    cg.relay()
    rg.relay()
    cg.near()
    rg.near()
    cg.far()
    rg.far()
    rg.rest()
    wire.drain()


def tile_kernel(first, last, *refs):
    refs = list(refs)
    rows, cols, count, where_at, tiles = refs[:5]
    refs = refs[5:]
    if not first:
        u, v, xrt, xc = refs[:4]
        refs = refs[4:]
    if not last:
        xr, xct = refs[:2]
        refs = refs[2:]
    if not first:
        omega_out = refs.pop(0)
    if last:
        grad_out = refs.pop(0)
    else:
        rp, cp, racc, cacc = refs
    step = pl.program_id(0)
    live = count[0]

    if not last:

        @pl.when(step == 0)
        def _():
            racc[...] = jnp.zeros_like(racc)
            cacc[...] = jnp.zeros_like(cacc)

    @pl.when(step * GROUP < live)
    def _():
        if not first:
            identity = lax.broadcasted_iota(jnp.int32, (128, 128), 0) == lax.broadcasted_iota(jnp.int32, (128, 128), 1)
        for j in range(GROUP):
            k = step * GROUP + j
            alive = k < live
            sr, sc = rows[k], cols[k]
            omega = jnp.where(alive, tiles[j], 0.0)
            if not first:
                left = jnp.dot(u[sr], xc[sc], preferred_element_type=F32)
                right = jnp.dot(xrt[sr], v[sc], preferred_element_type=F32)
                grad = jnp.where(alive, (left + right) * (0.5 / 256), 0.0)
                moved = omega - step_size * grad
                t = step_size * penalty
                shrunk = moved - jnp.clip(moved, -t, t)
                diagonal = 0.5 * (moved + jnp.sqrt(moved * moved + 4.0 * step_size))
                on = jnp.logical_and(identity, jnp.logical_and(alive, where_at[0] + sr == where_at[1] + sc))
                omega = jnp.where(on, diagonal, shrunk)
                omega_out[j] = omega
                if last:
                    grad_out[j] = grad
            if not last:
                low = omega.astype(BF16)
                racc[sr] += jnp.dot(low, xct[sc], preferred_element_type=F32)
                cacc[sc] += jnp.dot(xr[sr], low, preferred_element_type=F32)

    if not first:

        @pl.when(step * GROUP >= live)
        def _():
            omega_out[...] = jnp.zeros_like(omega_out)
            if last:
                grad_out[...] = jnp.zeros_like(grad_out)

    if not last:

        @pl.when(step == pl.num_programs(0) - 1)
        def _():
            rp[...] = racc[...].astype(BF16)
            cp[...] = cacc[...].astype(BF16)


def tile_call(first, last, scalars, tiles, dense):
    slots = tiles.shape[0]
    smem = pl.BlockSpec(memory_space=pltpu.SMEM)
    vmem = pl.BlockSpec(memory_space=pltpu.VMEM)
    block = pl.BlockSpec((GROUP, 128, 128), lambda i: (i, 0, 0))
    out_shape, out_specs, scratch = [], [], []
    if not first:
        out_shape.append(jax.ShapeDtypeStruct(tiles.shape, F32))
        out_specs.append(block)
    if last:
        out_shape.append(jax.ShapeDtypeStruct(tiles.shape, F32))
        out_specs.append(block)
    else:
        out_shape += [jax.ShapeDtypeStruct((32, 128, 256), BF16), jax.ShapeDtypeStruct((16, 256, 128), BF16)]
        out_specs += [vmem, vmem]
        scratch = [pltpu.VMEM((32, 128, 256), F32), pltpu.VMEM((16, 256, 128), F32)]
    return pl.pallas_call(
        functools.partial(tile_kernel, first, last),
        grid=(slots // GROUP,),
        out_shape=out_shape,
        in_specs=[smem] * 4 + [block] + [vmem] * len(dense),
        out_specs=out_specs,
        scratch_shapes=scratch,
        compiler_params=pltpu.CompilerParams(vmem_limit_bytes=LIMIT),
    )(*scalars, tiles, *dense)


def prep(counts, whiten):
    vmem = pl.BlockSpec(memory_space=pltpu.VMEM)
    n = 15 + 15 + 7
    shapes = ((16, 512, 128), (8, 512, 128), (16, 256, 256), (8, 256, 256))
    return pl.pallas_call(
        prep_kernel,
        out_shape=[jax.ShapeDtypeStruct(s, BF16) for s in shapes],
        in_specs=[vmem, pl.BlockSpec(memory_space=pl.ANY)],
        out_specs=[vmem] * 4,
        scratch_shapes=[
            pltpu.VMEM((8, 16, 512), jnp.int16),
            pltpu.VMEM((16, 16, 512), jnp.int16),
            pltpu.VMEM((512, 256), BF16),
            pltpu.SemaphoreType.DMA,
            pltpu.SemaphoreType.DMA((2,)),
            pltpu.SemaphoreType.DMA((n,)),
            pltpu.SemaphoreType.DMA((n,)),
        ],
        compiler_params=pltpu.CompilerParams(collective_id=0, has_side_effects=True, vmem_limit_bytes=LIMIT),
    )(counts, whiten)


def reduce_both(rp, cp, collective_id):
    vmem = pl.BlockSpec(memory_space=pltpu.VMEM)
    n = 8 + 7 + 7 + 15 + 7
    u, v = pl.pallas_call(
        reduce_kernel,
        out_shape=[jax.ShapeDtypeStruct((16, 256, 256), BF16), jax.ShapeDtypeStruct((8, 512, 128), BF16)],
        in_specs=[vmem] * 2,
        out_specs=[vmem] * 2,
        scratch_shapes=[
            pltpu.VMEM((8, 256, 256), BF16),
            pltpu.VMEM((8, 256, 256), BF16),
            pltpu.VMEM((6, 256, 256), BF16),
            pltpu.VMEM((256, 256), BF16),
            pltpu.VMEM((256, 256), F32),
            pltpu.VMEM((256, 256), BF16),
            pltpu.VMEM((6, 512, 128), BF16),
            pltpu.VMEM((512, 128), BF16),
            pltpu.VMEM((512, 128), F32),
            pltpu.VMEM((512, 128), BF16),
            pltpu.SemaphoreType.DMA((n,)),
            pltpu.SemaphoreType.DMA((n,)),
        ],
        compiler_params=pltpu.CompilerParams(
            collective_id=collective_id, has_side_effects=True, vmem_limit_bytes=LIMIT
        ),
    )(rp.reshape(16, 256, 256), cp.reshape(8, 512, 128))
    return u.reshape(32, 128, 256), v.reshape(16, 256, 128)


def local(counts, whiten, initial_tiles, tile_rows, tile_cols, tile_count):
    tiles = initial_tiles.reshape(96, 128, 128)
    where_at = jnp.stack([lax.axis_index("row") * 32, lax.axis_index("col") * 16]).astype(jnp.int32)
    scalars = (tile_rows.reshape(96), tile_cols.reshape(96), tile_count.reshape(1), where_at)
    xr, xc, xrt, xct = prep(counts, whiten)
    xr, xc = xr.reshape(32, 256, 128), xc.reshape(16, 256, 128)
    xrt, xct = xrt.reshape(32, 128, 256), xct.reshape(16, 128, 256)
    rp, cp = tile_call(True, False, scalars, tiles, (xr, xct))
    u, v = reduce_both(rp, cp, 1)
    omega, rp, cp = tile_call(False, False, scalars, tiles, (u, v, xrt, xc, xr, xct))
    u, v = reduce_both(rp, cp, 2)
    omega, grad = tile_call(False, True, scalars, omega, (u, v, xrt, xc))
    return omega.reshape(initial_tiles.shape), grad.reshape(initial_tiles.shape)


def solution(mesh):
    in_specs = (
        P("col", "row"),
        P("row", None, None),
        P("row", "col", None, None, None),
        P("row", "col", None),
        P("row", "col", None),
        P("row", "col"),
    )
    out_specs = (P("row", "col", None, None, None), P("row", "col", None, None, None))
    return jax.shard_map(local, mesh=mesh, in_specs=in_specs, out_specs=out_specs, check_vma=False)
```

```python
import functools

import jax
import jax.numpy as jnp
from jax import lax
from jax.experimental import pallas as pl
from jax.experimental.pallas import tpu as pltpu
from jax.sharding import PartitionSpec as P

step_size = 0.08
penalty = 1.0
epsilon = 1e-05
MESH = pl.DeviceIdType.MESH
F32 = jnp.float32
BF16 = jnp.bfloat16
GROUP = 8
MIB = 2**20
PREP_MIB = 39


class Place:
    def __init__(self):
        self.row = lax.axis_index("row")
        self.col = lax.axis_index("col")
        self.y, self.zh = self.row // 2, self.row % 2
        self.zl, self.x, self.core = self.col // 8, (self.col // 2) % 4, self.col % 2
        self.mine = self.core * 8 + self.x * 2 + self.zl
        self.mine_col = self.row

    def at(self, row=None, col=None):
        return (self.row if row is None else row, self.col if col is None else col)

    def xpeer(self, d):
        return self.at(col=self.zl * 8 + ((self.x + d) % 4) * 2 + self.core)

    def ypeer(self, d):
        return self.at(row=((self.y + d) % 4) * 2 + self.zh)

    def zlpeer(self):
        return self.at(col=(1 - self.zl) * 8 + self.x * 2 + self.core)

    def zhpeer(self):
        return self.at(row=self.y * 2 + 1 - self.zh)

    def sibling(self):
        return self.at(col=self.zl * 8 + self.x * 2 + 1 - self.core)


class Wire:
    def __init__(self, send_sem, recv_sem):
        self.send_sem, self.recv_sem = send_sem, recv_sem
        self.copies = {}

    def send(self, name, src, dst, device):
        i = len(self.copies)
        copy = pltpu.make_async_remote_copy(
            src_ref=src, dst_ref=dst, send_sem=self.send_sem.at[i],
            recv_sem=self.recv_sem.at[i], device_id=device, device_id_type=MESH,
        )
        copy.start()
        self.copies[name] = copy

    def recv(self, *names):
        for name in names:
            self.copies[name].wait_recv()

    def drain(self):
        for copy in self.copies.values():
            copy.wait_send()


class Gather:
    def __init__(self, wire, tag, out, base, position, z, ring, zpeer, sibling, done):
        self.w, self.tag, self.out = wire, tag, out
        self.base, self.position, self.z = base, position, z
        self.ring, self.zpeer, self.sibling, self.done = ring, zpeer, sibling, done

    def slot(self, d, other):
        z = 1 - self.z if other else self.z
        return self.base + ((self.position + d) % 4) * 2 + z

    def pass_on(self, name, slot, device):
        self.w.send(self.tag + name, self.out.at[slot], self.out.at[slot], device)

    def have(self, name, slot):
        if self.sibling is not None:
            self.pass_on("core" + name, slot, self.sibling)

    def own(self):
        s = self.slot(0, False)
        self.pass_on("z", s, self.zpeer)
        self.pass_on("own+", s, self.ring(1))
        self.pass_on("own-", s, self.ring(3))
        self.have("own", s)
        self.done(s)

    def other(self):
        s = self.slot(0, True)
        self.w.recv(self.tag + "z")
        self.pass_on("other+", s, self.ring(1))
        self.pass_on("other-", s, self.ring(3))
        self.have("other", s)
        self.done(s)

    def relay(self):
        left, right = self.slot(3, False), self.slot(1, True)
        self.w.recv(self.tag + "own+")
        self.pass_on("far+", left, self.ring(1))
        self.have("a", left)
        self.w.recv(self.tag + "other-")
        self.pass_on("far-", right, self.ring(3))
        self.have("b", right)
        self.done(left)
        self.done(right)

    def near(self):
        left, right = self.slot(3, True), self.slot(1, False)
        self.w.recv(self.tag + "own-")
        self.have("c", right)
        self.w.recv(self.tag + "other+")
        self.have("d", left)
        self.done(right)
        self.done(left)

    def far(self):
        a, b = self.slot(2, False), self.slot(2, True)
        self.w.recv(self.tag + "far+")
        self.have("e", a)
        self.w.recv(self.tag + "far-")
        self.have("f", b)
        self.done(a)
        self.done(b)

    def rest(self):
        if self.sibling is None:
            return
        flip = 8 - 2 * self.base
        for name, d, other in (
            ("own", 0, 0), ("other", 0, 1), ("a", 3, 0), ("b", 1, 1),
            ("c", 1, 0), ("d", 3, 1), ("e", 2, 0), ("f", 2, 1),
        ):
            self.w.recv(self.tag + "core" + name)
            self.done(self.slot(d, other) + flip)


def row_gather(wire, place, out, done):
    return Gather(wire, "r", out, place.core * 8, place.x, place.zl, place.xpeer, place.zlpeer(), place.sibling(), done)


def col_gather(wire, place, out, done):
    return Gather(wire, "c", out, 0, place.y, place.zh, place.ypeer, place.zhpeer(), None, done)


def greet(devices):
    barrier = pltpu.get_barrier_semaphore()
    for device in devices:
        pl.semaphore_signal(barrier, inc=1, device_id=device, device_id_type=MESH)
    return barrier


def prep_kernel(
    counts_hbm, tiles_hbm, whiten, xr, xc, xrt, xct, tiles, counts, packed, landed, wsem, lsem, send_sem, recv_sem
):
    place = Place()
    block = place.mine // 2
    to_row, to_col = place.x * 2 + place.zl, 2 * place.row + place.core
    from_row, from_col = place.col // 2, (place.row % 2) * 8 + (place.row // 2) * 2 + place.core
    moves = jnp.logical_or(to_row != place.row, to_col != place.col)
    peers = [place.at(col=(place.col + d) % 16) for d in range(1, 16)]
    peers += [place.ypeer(d) for d in (1, 3)] + [place.zhpeer()]
    barrier = greet(peers)

    @pl.when(moves)
    def _():
        for device in ((to_row, to_col), (from_row, from_col)):
            pl.semaphore_signal(barrier, inc=1, device_id=device, device_id_type=MESH)

    counted = pltpu.make_async_copy(counts_hbm, counts, wsem.at[0])
    tiled = pltpu.make_async_copy(tiles_hbm, tiles, wsem.at[1])
    counted.start()
    tiled.start()
    counted.wait()
    for b in range(8):
        packed[b] = counts[:, b * 512 : (b + 1) * 512].astype(jnp.int16)
    pl.semaphore_wait(barrier, len(peers) + 2 * moves.astype(jnp.int32))

    wire = Wire(send_sem, recv_sem)
    for d in range(1, 16):
        c = (place.col + d) % 16
        b = (c % 2) * 4 + (c // 2) % 4
        wire.send(f"a{d}", packed.at[b], landed.at[place.col], place.at(col=c))
    landed[place.col] = packed[block]
    wire.recv(*[f"a{d}" for d in range(1, 16)])
    logged = jnp.log(1.0 + landed[...].astype(jnp.int32).astype(F32)).reshape(256, 512)
    mean = jnp.mean(logged, axis=0, keepdims=True)
    centered = logged - mean
    variance = jnp.mean(centered * centered, axis=0, keepdims=True)
    standard = (centered * lax.rsqrt(variance + epsilon)).astype(BF16)
    whitened = jnp.dot(standard, whiten[...], preferred_element_type=F32).astype(BF16)
    xr[place.mine, :256] = whitened[:, :128]
    xr[place.mine, 256:] = whitened[:, 128:]

    def turn(source, target):
        def done(s):
            target[s, :128] = source[s, :256].T
            target[s, 128:] = source[s, 256:].T

        return done

    row = row_gather(wire, place, xr, turn(xr, xrt))
    col = col_gather(wire, place, xc, turn(xc, xct))
    hop = pltpu.make_async_remote_copy(
        src_ref=xr.at[place.mine], dst_ref=xc.at[to_row], send_sem=lsem.at[0],
        recv_sem=lsem.at[1], device_id=(to_row, to_col), device_id_type=MESH,
    )

    @pl.when(moves)
    def _():
        hop.start()

    @pl.when(jnp.logical_not(moves))
    def _():
        xc[place.mine_col] = xr[place.mine]

    row.own()

    @pl.when(moves)
    def _():
        hop.wait_recv()

    col.own()
    row.other()
    col.other()
    row.relay()
    col.relay()
    row.near()
    col.near()
    row.far()
    col.far()
    row.rest()
    tiled.wait()
    wire.drain()

    @pl.when(moves)
    def _():
        hop.wait_send()


def add(*parts):
    total = parts[0].astype(F32)
    for part in parts[1:]:
        total = total + part.astype(F32)
    return total


class Scatter:
    def __init__(self, wire, tag, land, zland, keep, zout, z, ring, zpeer, pick, stage):
        self.w, self.tag, self.land, self.zland = wire, tag, land, zland
        self.keep, self.zout, self.z = keep, zout, z
        self.ring, self.zpeer, self.pick, self.stage = ring, zpeer, pick, stage

    def put(self, name, i, src, device):
        self.w.send(self.tag + name, src, self.land.at[i], device)

    def first(self):
        self.put("A1", 0, self.stage(2, 0), self.ring(1))
        self.put("B1", 1, self.stage(2, 1), self.ring(3))

    def second(self):
        self.put("A2", 2, self.stage(1, 1), self.ring(1))
        self.put("B2", 3, self.stage(3, 0), self.ring(3))

    def merge(self):
        self.w.recv(self.tag + "A1")
        self.land[0] = add(self.pick(1, 0), self.land[0]).astype(BF16)
        self.put("A3", 4, self.land.at[0], self.ring(1))
        self.w.recv(self.tag + "B1")
        self.land[1] = add(self.pick(3, 1), self.land[1]).astype(BF16)
        self.put("B3", 5, self.land.at[1], self.ring(3))

    def cross(self):
        self.w.recv(*[self.tag + n for n in ("B2", "A2", "A3", "B3")])
        own = (add(self.pick(0, 0), self.land[3], self.land[4]), add(self.pick(0, 1), self.land[2], self.land[5]))
        mine = self.z == 0
        self.zout[...] = jnp.where(mine, own[1], own[0]).astype(BF16)
        self.w.send(self.tag + "Z", self.zout, self.zland, self.zpeer)
        self.keep[...] = jnp.where(mine, own[0], own[1])

    def last(self, out, slot):
        self.w.recv(self.tag + "Z")
        out[slot] = add(self.keep[...], self.zland[...]).astype(BF16)


def reduce_kernel(
    rp, cp, u, v, pair, summed, rland, rzland, rkeep, rzout, cland, czland, ckeep, czout, send_sem, recv_sem
):
    place = Place()
    peers = [place.sibling(), place.xpeer(1), place.xpeer(3), place.zlpeer()]
    peers += [place.ypeer(1), place.ypeer(3), place.zhpeer()]
    barrier = greet(peers)
    pl.semaphore_wait(barrier, len(peers))
    wire = Wire(send_sem, recv_sem)
    here, there = place.core * 8, 8 - place.core * 8

    def rslot(d, e):
        return ((place.x + d) % 4) * 2 + e

    def cslot(d, e):
        return ((place.y + d) % 4) * 2 + e

    order = ((2, 0), (2, 1), (1, 1), (3, 0), (1, 0), (3, 1), (0, 0), (0, 1))
    for d, e in order:
        s = rslot(d, e)
        wire.send(f"s{d}{e}", rp.at[there + s], pair.at[s], place.sibling())
    col = Scatter(
        wire, "cs", cland, czland, ckeep, czout, place.zh, place.ypeer, place.zhpeer(),
        lambda d, e: cp[cslot(d, e)], lambda d, e: cp.at[cslot(d, e)],
    )
    row = Scatter(
        wire, "rs", rland, rzland, rkeep, rzout, place.zl, place.xpeer, place.zlpeer(),
        lambda d, e: summed[rslot(d, e)], lambda d, e: summed.at[rslot(d, e)],
    )
    col.first()
    col.second()

    def join(d, e):
        s = rslot(d, e)
        wire.recv(f"s{d}{e}")
        summed[s] = add(rp[here + s], pair[s]).astype(BF16)

    for d, e in order[:2]:
        join(d, e)
    row.first()
    for d, e in order[2:4]:
        join(d, e)
    row.second()
    for d, e in order[4:]:
        join(d, e)
    col.merge()
    row.merge()
    col.cross()
    row.cross()
    nothing = lambda s: None
    rg = row_gather(wire, place, u, nothing)
    cg = col_gather(wire, place, v, nothing)
    col.last(v, place.mine_col)
    cg.own()
    row.last(u, place.mine)
    rg.own()
    cg.other()
    rg.other()
    cg.relay()
    rg.relay()
    cg.near()
    rg.near()
    cg.far()
    rg.far()
    rg.rest()
    wire.drain()


def live_groups(count):
    return (count[0] + GROUP - 1) // GROUP


def gradient(k, live, rows, cols, u, v, xrt, xc):
    sr, sc = rows[k], cols[k]
    left = jnp.dot(u[sr], xc[sc], preferred_element_type=F32)
    right = jnp.dot(xrt[sr], v[sc], preferred_element_type=F32)
    return jnp.where(k < live, (left + right) * (0.5 / 256), 0.0)


def moved_to(k, live, rows, cols, where_at, identity, omega, grad):
    moved = omega - step_size * grad
    t = step_size * penalty
    shrunk = moved - jnp.clip(moved, -t, t)
    diagonal = 0.5 * (moved + jnp.sqrt(moved * moved + 4.0 * step_size))
    on = jnp.logical_and(k < live, where_at[0] + rows[k] == where_at[1] + cols[k])
    return jnp.where(jnp.logical_and(identity, on), diagonal, shrunk)


def eye():
    return lax.broadcasted_iota(jnp.int32, (128, 128), 0) == lax.broadcasted_iota(jnp.int32, (128, 128), 1)


def products(k, low, rows, cols, xr, xct, racc, cacc):
    sr, sc = rows[k], cols[k]
    racc[sr] += jnp.dot(low, xct[sc], preferred_element_type=F32)
    cacc[sc] += jnp.dot(xr[sr], low, preferred_element_type=F32)


def first_kernel(rows, cols, count, where_at, tiles, xr, xct, rp, cp, racc, cacc):
    racc[...] = jnp.zeros_like(racc)
    cacc[...] = jnp.zeros_like(cacc)
    live = count[0]

    def group(g, _):
        for j in range(GROUP):
            k = g * GROUP + j
            low = jnp.where(k < live, tiles[k], 0.0).astype(BF16)
            products(k, low, rows, cols, xr, xct, racc, cacc)
        return 0

    lax.fori_loop(0, live_groups(count), group, 0)
    rp[...] = racc[...].astype(BF16)
    cp[...] = cacc[...].astype(BF16)


def middle_kernel(
    rows, cols, count, where_at, tiles, u, v, xrt, xc, xr, xct, omega_out, rp, cp, racc, cacc, low
):
    racc[...] = jnp.zeros_like(racc)
    cacc[...] = jnp.zeros_like(cacc)
    live = count[0]

    def group(g, _):
        identity = eye()
        for j in range(GROUP):
            k = g * GROUP + j
            grad = gradient(k, live, rows, cols, u, v, xrt, xc)
            omega = jnp.where(k < live, tiles[k], 0.0)
            omega = moved_to(k, live, rows, cols, where_at, identity, omega, grad)
            omega_out[k] = omega
            low[j] = omega.astype(BF16)
        for j in range(GROUP):
            products(g * GROUP + j, low[j], rows, cols, xr, xct, racc, cacc)
        return 0

    lax.fori_loop(0, live_groups(count), group, 0)
    rp[...] = racc[...].astype(BF16)
    cp[...] = cacc[...].astype(BF16)


def last_kernel(rows, cols, count, where_at, tiles, u, v, xrt, xc, omega_out, grad_out, obuf, gbuf, zeros, sem):
    live = count[0]
    groups, total = live_groups(count), omega_out.shape[0] // GROUP

    def writes(g, o, d):
        here = pl.ds(g * GROUP, GROUP)
        return (
            pltpu.make_async_copy(o, omega_out.at[here], sem.at[0, g]),
            pltpu.make_async_copy(d, grad_out.at[here], sem.at[1, g]),
        )

    zeros[...] = jnp.zeros_like(zeros)

    def dead(g, _):
        for copy in writes(g, zeros, zeros):
            copy.start()
        return 0

    lax.fori_loop(groups, total, dead, 0)

    def group(g, _):
        identity = eye()
        for j in range(GROUP):
            k = g * GROUP + j
            grad = gradient(k, live, rows, cols, u, v, xrt, xc)
            omega = jnp.where(k < live, tiles[k], 0.0)
            gbuf[k] = grad
            obuf[k] = moved_to(k, live, rows, cols, where_at, identity, omega, grad)
        here = pl.ds(g * GROUP, GROUP)
        for copy in writes(g, obuf.at[here], gbuf.at[here]):
            copy.start()
        return 0

    lax.fori_loop(0, groups, group, 0)

    def wait(g, _):
        for copy in writes(g, zeros, zeros):
            copy.wait()
        return 0

    lax.fori_loop(0, total, wait, 0)


def tile_call(kernel, scalars, dense, out_shape, out_space, scratch, limit):
    smem = pl.BlockSpec(memory_space=pltpu.SMEM)
    vmem = pl.BlockSpec(memory_space=pltpu.VMEM)
    return pl.pallas_call(
        kernel,
        out_shape=out_shape,
        in_specs=[smem] * 4 + [vmem] * len(dense),
        out_specs=[pl.BlockSpec(memory_space=out_space)] * len(out_shape),
        scratch_shapes=scratch,
        compiler_params=pltpu.CompilerParams(vmem_limit_bytes=limit * MIB),
    )(*scalars, *dense)


def prep(counts, whiten, tiles):
    mine = Place().mine
    whiten = lax.dynamic_slice(whiten, (mine // 2, 0, mine % 2 * 256), (1, 512, 256)).reshape(512, 256)
    vmem = pl.BlockSpec(memory_space=pltpu.VMEM)
    n = 15 + 15 + 7
    shapes = ((16, 512, 128), (8, 512, 128), (16, 256, 256), (8, 256, 256))
    return pl.pallas_call(
        prep_kernel,
        out_shape=[jax.ShapeDtypeStruct(s, BF16) for s in shapes] + [jax.ShapeDtypeStruct(tiles.shape, F32)],
        in_specs=[pl.BlockSpec(memory_space=pltpu.HBM)] * 2 + [vmem],
        out_specs=[vmem] * 5,
        scratch_shapes=[
            pltpu.VMEM((16, 4096), jnp.int32),
            pltpu.VMEM((8, 16, 512), jnp.int16),
            pltpu.VMEM((16, 16, 512), jnp.int16),
            pltpu.SemaphoreType.DMA((2,)),
            pltpu.SemaphoreType.DMA((2,)),
            pltpu.SemaphoreType.DMA((n,)),
            pltpu.SemaphoreType.DMA((n,)),
        ],
        compiler_params=pltpu.CompilerParams(collective_id=0, has_side_effects=True, vmem_limit_bytes=PREP_MIB * MIB),
    )(counts, tiles, whiten)


def reduce_both(rp, cp, collective_id):
    vmem = pl.BlockSpec(memory_space=pltpu.VMEM)
    n = 8 + 7 + 7 + 15 + 7
    u, v = pl.pallas_call(
        reduce_kernel,
        out_shape=[jax.ShapeDtypeStruct((16, 256, 256), BF16), jax.ShapeDtypeStruct((8, 512, 128), BF16)],
        in_specs=[vmem] * 2,
        out_specs=[vmem] * 2,
        scratch_shapes=[
            pltpu.VMEM((8, 256, 256), BF16),
            pltpu.VMEM((8, 256, 256), BF16),
            pltpu.VMEM((6, 256, 256), BF16),
            pltpu.VMEM((256, 256), BF16),
            pltpu.VMEM((256, 256), F32),
            pltpu.VMEM((256, 256), BF16),
            pltpu.VMEM((6, 512, 128), BF16),
            pltpu.VMEM((512, 128), BF16),
            pltpu.VMEM((512, 128), F32),
            pltpu.VMEM((512, 128), BF16),
            pltpu.SemaphoreType.DMA((n,)),
            pltpu.SemaphoreType.DMA((n,)),
        ],
        compiler_params=pltpu.CompilerParams(
            collective_id=collective_id, has_side_effects=True, vmem_limit_bytes=12 * MIB
        ),
    )(rp.reshape(16, 256, 256), cp.reshape(8, 512, 128))
    return u.reshape(32, 128, 256), v.reshape(16, 256, 128)


def local(counts, whiten, initial_tiles, tile_rows, tile_cols, tile_count):
    where_at = jnp.stack([lax.axis_index("row") * 32, lax.axis_index("col") * 16]).astype(jnp.int32)
    scalars = (tile_rows.reshape(96), tile_cols.reshape(96), tile_count.reshape(1), where_at)
    xr, xc, xrt, xct, tiles = prep(counts, whiten, initial_tiles.reshape(96, 128, 128))
    xr, xc = xr.reshape(32, 256, 128), xc.reshape(16, 256, 128)
    xrt, xct = xrt.reshape(32, 128, 256), xct.reshape(16, 128, 256)
    omega_shape = jax.ShapeDtypeStruct(tiles.shape, F32)
    part_shapes = [jax.ShapeDtypeStruct((32, 128, 256), BF16), jax.ShapeDtypeStruct((16, 256, 128), BF16)]
    sums = [pltpu.VMEM((32, 128, 256), F32), pltpu.VMEM((16, 256, 128), F32)]
    rp, cp = tile_call(first_kernel, scalars, (tiles, xr, xct), part_shapes, pltpu.VMEM, sums, 12)
    u, v = reduce_both(rp, cp, 1)
    omega, rp, cp = tile_call(
        middle_kernel, scalars, (tiles, u, v, xrt, xc, xr, xct), [omega_shape] + part_shapes, pltpu.VMEM,
        sums + [pltpu.VMEM((GROUP, 128, 128), BF16)], 12,
    )
    u, v = reduce_both(rp, cp, 2)
    buffers = [pltpu.VMEM(tiles.shape, F32)] * 2 + [pltpu.VMEM((GROUP, 128, 128), F32)]
    omega, grad = tile_call(
        last_kernel, scalars, (omega, u, v, xrt, xc), [omega_shape] * 2, pltpu.HBM,
        buffers + [pltpu.SemaphoreType.DMA((2, 96 // GROUP))], 20,
    )
    return omega.reshape(initial_tiles.shape), grad.reshape(initial_tiles.shape)


def solution(mesh):
    in_specs = (
        P("col", "row"),
        P("row", None, None),
        P("row", "col", None, None, None),
        P("row", "col", None),
        P("row", "col", None),
        P("row", "col"),
    )
    out_specs = (P("row", "col", None, None, None), P("row", "col", None, None, None))
    return jax.shard_map(local, mesh=mesh, in_specs=in_specs, out_specs=out_specs, check_vma=False)
```

```python
import functools

import jax
import jax.numpy as jnp
from jax import lax
from jax.experimental import pallas as pl
from jax.experimental.pallas import tpu as pltpu
from jax.sharding import PartitionSpec as P

step_size = 0.08
penalty = 1.0
epsilon = 1e-05
MESH = pl.DeviceIdType.MESH
F32 = jnp.float32
BF16 = jnp.bfloat16
GROUP = 8
MIB = 2**20
PREP_MIB = 39


class Place:
    def __init__(self):
        self.row = lax.axis_index("row")
        self.col = lax.axis_index("col")
        self.y, self.zh = self.row // 2, self.row % 2
        self.zl, self.x, self.core = self.col // 8, (self.col // 2) % 4, self.col % 2
        self.mine = self.core * 8 + self.x * 2 + self.zl
        self.mine_col = self.row

    def at(self, row=None, col=None):
        return (self.row if row is None else row, self.col if col is None else col)

    def xpeer(self, d):
        return self.at(col=self.zl * 8 + ((self.x + d) % 4) * 2 + self.core)

    def ypeer(self, d):
        return self.at(row=((self.y + d) % 4) * 2 + self.zh)

    def zlpeer(self):
        return self.at(col=(1 - self.zl) * 8 + self.x * 2 + self.core)

    def zhpeer(self):
        return self.at(row=self.y * 2 + 1 - self.zh)

    def sibling(self):
        return self.at(col=self.zl * 8 + self.x * 2 + 1 - self.core)


class Wire:
    def __init__(self, send_sem, recv_sem):
        self.send_sem, self.recv_sem = send_sem, recv_sem
        self.copies = {}

    def send(self, name, src, dst, device):
        i = len(self.copies)
        copy = pltpu.make_async_remote_copy(
            src_ref=src, dst_ref=dst, send_sem=self.send_sem.at[i],
            recv_sem=self.recv_sem.at[i], device_id=device, device_id_type=MESH,
        )
        copy.start()
        self.copies[name] = copy

    def recv(self, *names):
        for name in names:
            self.copies[name].wait_recv()

    def drain(self):
        for copy in self.copies.values():
            copy.wait_send()


class Stream:
    def __init__(self, part, parts):
        self.part, self.parts = part, parts

    def rows(self, ref):
        size = ref.shape[-2] // self.parts
        return pl.ds(self.part * size, size)

    def cut(self, ref, i):
        return ref.at[i, self.rows(ref)]


class Gather:
    def __init__(self, wire, stream, tag, out, base, position, z, ring, sibling, done, relayed):
        self.w, self.stream, self.tag, self.out = wire, stream, f"{tag}{stream.part}", out
        self.base, self.position, self.z = base, position, z
        self.ring, self.sibling, self.done, self.relayed = ring, sibling, done, relayed
        self.shared = []

    def slot(self, d, other):
        z = 1 - self.z if other else self.z
        return self.base + ((self.position + d) % 4) * 2 + z

    def pass_on(self, name, slot, device):
        part = self.stream.cut(self.out, slot)
        self.w.send(f"{self.tag}{name}", part, part, device)

    def have(self, d, other):
        s = self.slot(d, other)
        if self.sibling is not None:
            self.pass_on(f"core{d}{other}", s, self.sibling)
            self.shared.append((d, other))
        self.done(s)

    def exchange(self, zpeer):
        self.pass_on("z", self.slot(0, 0), zpeer)

    def exchanged(self):
        self.w.recv(self.tag + "z")

    def start(self, other):
        for d in (1, 3) if self.relayed else (1, 3, 2):
            self.pass_on(f"{other}{d}", self.slot(0, other), self.ring(d))
        self.have(0, other)

    def arrive(self, other, d):
        self.w.recv(f"{self.tag}{other}{d}")
        if self.relayed and (other, d) in ((0, 1), (1, 3)):
            self.pass_on(f"{other}2", self.slot(4 - d, other), self.ring(d))
        self.have(4 - d, other)

    def rest(self):
        for d, other in self.shared:
            self.w.recv(f"{self.tag}core{d}{other}")
            self.done(self.slot(d, other) + 8 - 2 * self.base)


def arrivals(gathers):
    for other in (0, 1):
        for d in (1, 3, 2):
            for gather in gathers:
                gather.arrive(other, d)
    for gather in gathers:
        gather.rest()


def row_gather(wire, stream, place, out, done, relayed):
    return Gather(
        wire, stream, "r", out, place.core * 8, place.x, place.zl, place.xpeer, place.sibling(), done, relayed
    )


def col_gather(wire, stream, place, out, done, relayed):
    return Gather(wire, stream, "c", out, 0, place.y, place.zh, place.ypeer, None, done, relayed)


PARTS = 2


def greet(devices):
    barrier = pltpu.get_barrier_semaphore()
    for device in devices:
        pl.semaphore_signal(barrier, inc=1, device_id=device, device_id_type=MESH)
    return barrier


def prep_kernel(
    counts_hbm, tiles_hbm, whiten, xr, xc, xrt, xct, tiles, counts, packed, landed, wsem, lsem, send_sem, recv_sem
):
    place = Place()
    block = place.mine // 2
    to_row, to_col = place.x * 2 + place.zl, 2 * place.row + place.core
    from_row, from_col = place.col // 2, (place.row % 2) * 8 + (place.row // 2) * 2 + place.core
    moves = jnp.logical_or(to_row != place.row, to_col != place.col)
    peers = [place.at(col=(place.col + d) % 16) for d in range(1, 16)]
    peers += [place.ypeer(d) for d in (1, 2, 3)] + [place.zhpeer()]
    barrier = greet(peers)

    @pl.when(moves)
    def _():
        for device in ((to_row, to_col), (from_row, from_col)):
            pl.semaphore_signal(barrier, inc=1, device_id=device, device_id_type=MESH)

    counted = pltpu.make_async_copy(counts_hbm, counts, wsem.at[0])
    tiled = pltpu.make_async_copy(tiles_hbm, tiles, wsem.at[1])
    counted.start()
    tiled.start()
    counted.wait()
    for b in range(8):
        packed[b] = counts[:, b * 512 : (b + 1) * 512].astype(jnp.int16)
    pl.semaphore_wait(barrier, len(peers) + 2 * moves.astype(jnp.int32))

    wire = Wire(send_sem, recv_sem)
    for d in range(1, 16):
        c = (place.col + d) % 16
        b = (c % 2) * 4 + (c // 2) % 4
        wire.send(f"a{d}", packed.at[b], landed.at[place.col], place.at(col=c))
    landed[place.col] = packed[block]
    wire.recv(*[f"a{d}" for d in range(1, 16)])
    logged = jnp.log(1.0 + landed[...].astype(jnp.int32).astype(F32)).reshape(256, 512)
    mean = jnp.mean(logged, axis=0, keepdims=True)
    centered = logged - mean
    variance = jnp.mean(centered * centered, axis=0, keepdims=True)
    standard = (centered * lax.rsqrt(variance + epsilon)).astype(BF16)
    whitened = jnp.dot(standard, whiten[...], preferred_element_type=F32).astype(BF16)
    pair = block * 2
    for j in range(4):
        xr[pair + j // 2, j % 2 * 256 : (j % 2 + 1) * 256] = whitened[:, j * 128 : (j + 1) * 128]

    def turn(source, target, part):
        def done(s):
            for t in range(2 // PARTS * part, 2 // PARTS * (part + 1)):
                target[s, t * 128 : (t + 1) * 128] = source[s, t * 256 : (t + 1) * 256].T

        return done

    streams = [Stream(p, PARTS) for p in range(PARTS)]
    rows = [row_gather(wire, t, place, xr, turn(xr, xrt, t.part), True) for t in streams]
    cols = [col_gather(wire, t, place, xc, turn(xc, xct, t.part), True) for t in streams]
    hop = pltpu.make_async_remote_copy(
        src_ref=xr.at[place.mine], dst_ref=xc.at[to_row], send_sem=lsem.at[0],
        recv_sem=lsem.at[1], device_id=(to_row, to_col), device_id_type=MESH,
    )

    @pl.when(moves)
    def _():
        hop.start()

    @pl.when(jnp.logical_not(moves))
    def _():
        xc[place.mine_col] = xr[place.mine]

    for row in rows:
        row.start(0)
        row.start(1)

    @pl.when(moves)
    def _():
        hop.wait_recv()

    for col in cols:
        col.exchange(place.zhpeer())
        col.start(0)
    for row in rows:
        row.arrive(0, 1)
        row.arrive(1, 3)
    for col in cols:
        col.arrive(0, 1)
        col.exchanged()
        col.start(1)
    for col in cols:
        col.arrive(0, 3)
    for other, d in ((0, 3), (1, 1), (0, 2), (1, 2)):
        for row in rows:
            row.arrive(other, d)
    for other, d in ((1, 3), (1, 1), (0, 2), (1, 2)):
        for col in cols:
            col.arrive(other, d)
    for row in rows:
        row.rest()
    tiled.wait()
    wire.drain()

    @pl.when(moves)
    def _():
        hop.wait_send()


def add(*parts):
    total = parts[0].astype(F32)
    for part in parts[1:]:
        total = total + part.astype(F32)
    return total


class Scatter:
    def __init__(self, wire, stream, tag, terms, slot, land, ztemp, keep, z, ring, zpeer):
        self.w, self.stream, self.tag = wire, stream, f"{tag}{stream.part}"
        self.terms, self.slot, self.land, self.ztemp, self.keep = terms, slot, land, ztemp, keep
        self.z, self.ring, self.zpeer = z, ring, zpeer

    def term(self, d, e):
        return self.stream.cut(self.terms, self.slot(d, e))

    def landed(self, i):
        return self.stream.cut(self.land, i)

    def put(self, name, i, src, device):
        self.w.send(self.tag + name, src, self.landed(i), device)

    def first(self):
        self.put("A1", 0, self.term(2, 0), self.ring(1))
        self.put("B1", 1, self.term(2, 1), self.ring(3))

    def second(self):
        self.put("A2", 2, self.term(1, 1), self.ring(1))
        self.put("B2", 3, self.term(3, 0), self.ring(3))

    def merge(self):
        for name, i, d, e, then in (("A1", 0, 1, 0, "A3"), ("B1", 1, 3, 1, "B3")):
            self.w.recv(self.tag + name)
            here = self.landed(i)
            here[...] = add(self.term(d, e)[...], here[...]).astype(BF16)
            self.put(then, 4 + i, here, self.ring(d))

    def cross(self):
        self.w.recv(*[self.tag + n for n in ("B2", "A2", "A3", "B3")])
        own = [
            add(self.term(0, e)[...], self.landed(i)[...], self.landed(j)[...]) for e, i, j in ((0, 3, 4), (1, 2, 5))
        ]
        mine = self.z == 0
        out = self.stream.cut(self.ztemp, 0)
        out[...] = jnp.where(mine, own[1], own[0]).astype(BF16)
        self.w.send(self.tag + "Z", out, self.stream.cut(self.ztemp, 1), self.zpeer)
        self.keep[self.stream.rows(self.keep)] = jnp.where(mine, own[0], own[1])

    def last(self, out, slot):
        self.w.recv(self.tag + "Z")
        got = self.stream.cut(self.ztemp, 1)[...]
        self.stream.cut(out, slot)[...] = add(self.keep[self.stream.rows(self.keep)], got).astype(BF16)


def reduce_kernel(rfull, cfull, u, v, rp, cp, pair, summed, rland, rtemp, rkeep, cland, ctemp, ckeep, send_sem, recv_sem):
    place = Place()
    peers = [place.sibling(), place.zlpeer(), place.zhpeer()]
    peers += [place.xpeer(d) for d in (1, 2, 3)] + [place.ypeer(d) for d in (1, 2, 3)]
    barrier = greet(peers)
    rp[...] = rfull[...].astype(BF16)
    cp[...] = cfull[...].astype(BF16)
    pl.semaphore_wait(barrier, len(peers))
    wire = Wire(send_sem, recv_sem)
    here, there = place.core * 8, 8 - place.core * 8

    def rslot(d, e):
        return ((place.x + d) % 4) * 2 + e

    def cslot(d, e):
        return ((place.y + d) % 4) * 2 + e

    streams = [Stream(p, PARTS) for p in range(PARTS)]
    cols = [
        Scatter(wire, t, "cs", cp, cslot, cland, ctemp, ckeep, place.zh, place.ypeer, place.zhpeer()) for t in streams
    ]
    rows = [
        Scatter(wire, t, "rs", summed, rslot, rland, rtemp, rkeep, place.zl, place.xpeer, place.zlpeer())
        for t in streams
    ]
    order = ((2, 0), (2, 1), (1, 1), (3, 0), (1, 0), (3, 1), (0, 0), (0, 1))
    for t in streams:
        for d, e in order:
            s = rslot(d, e)
            wire.send(f"s{t.part}{d}{e}", t.cut(rp, there + s), t.cut(pair, s), place.sibling())
    for col in cols:
        col.first()
        col.second()

    def join(t, which):
        for d, e in which:
            s = rslot(d, e)
            wire.recv(f"s{t.part}{d}{e}")
            t.cut(summed, s)[...] = add(t.cut(rp, here + s)[...], t.cut(pair, s)[...]).astype(BF16)

    for t, row in zip(streams, rows):
        join(t, order[:2])
        row.first()
        join(t, order[2:4])
        row.second()
    for t, row, col in zip(streams, rows, cols):
        col.merge()
        join(t, order[4:6])
        row.merge()
    for t in streams:
        join(t, order[6:])
    for row, col in zip(rows, cols):
        col.cross()
        row.cross()
    nothing = lambda s: None
    rgs = [row_gather(wire, t, place, u, nothing, False) for t in streams]
    cgs = [col_gather(wire, t, place, v, nothing, False) for t in streams]
    for row, col, rg, cg in zip(rows, cols, rgs, cgs):
        col.last(v, place.mine_col)
        cg.exchange(place.zhpeer())
        cg.start(0)
        row.last(u, place.mine)
        rg.exchange(place.zlpeer())
        rg.start(0)
    for rg, cg in zip(rgs, cgs):
        cg.exchanged()
        cg.start(1)
        rg.exchanged()
        rg.start(1)
    arrivals(cgs + rgs)
    wire.drain()


def live_groups(count):
    return (count[0] + GROUP - 1) // GROUP


def gradient(k, live, rows, cols, u, v, xrt, xc):
    sr, sc = rows[k], cols[k]
    left = jnp.dot(u[sr], xc[sc], preferred_element_type=F32)
    right = jnp.dot(xrt[sr], v[sc], preferred_element_type=F32)
    return jnp.where(k < live, (left + right) * (0.5 / 256), 0.0)


def shrunk(moved):
    t = step_size * penalty
    return moved - jnp.clip(moved, -t, t)


def fix_diagonal(g, live, rows, cols, where_at, grads, base, tiles, omega_out):
    for j in range(GROUP):
        k = g * GROUP + j

        @pl.when(jnp.logical_and(k < live, where_at[0] + rows[k] == where_at[1] + cols[k]))
        def _():
            moved = tiles[k] - step_size * grads[base + j]
            diagonal = 0.5 * (moved + jnp.sqrt(moved * moved + 4.0 * step_size))
            row = lax.broadcasted_iota(jnp.int32, (128, 128), 0)
            col = lax.broadcasted_iota(jnp.int32, (128, 128), 1)
            omega_out[k] = jnp.where(row == col, diagonal, omega_out[k])


def products(k, low, rows, cols, xr, xct, rp, cp):
    sr, sc = rows[k], cols[k]
    rp[sr] += jnp.dot(low, xct[sc], preferred_element_type=F32)
    cp[sc] += jnp.dot(xr[sr], low, preferred_element_type=F32)


def first_kernel(rows, cols, count, where_at, tiles, xr, xct, rp, cp):
    rp[...] = jnp.zeros_like(rp)
    cp[...] = jnp.zeros_like(cp)
    live = count[0]

    def group(g, _):
        for j in range(GROUP):
            k = g * GROUP + j
            low = jnp.where(k < live, tiles[k], 0.0).astype(BF16)
            products(k, low, rows, cols, xr, xct, rp, cp)
        return 0

    lax.fori_loop(0, live_groups(count), group, 0)


def middle_kernel(rows, cols, count, where_at, tiles, u, v, xrt, xc, xr, xct, omega_out, rp, cp, grads):
    rp[...] = jnp.zeros_like(rp)
    cp[...] = jnp.zeros_like(cp)
    live = count[0]

    def group(g, _):
        for j in range(GROUP):
            k = g * GROUP + j
            grad = gradient(k, live, rows, cols, u, v, xrt, xc)
            grads[j] = grad
            omega_out[k] = shrunk(jnp.where(k < live, tiles[k], 0.0) - step_size * grad)
        fix_diagonal(g, live, rows, cols, where_at, grads, 0, tiles, omega_out)
        for j in range(GROUP):
            k = g * GROUP + j
            products(k, omega_out[k].astype(BF16), rows, cols, xr, xct, rp, cp)
        return 0

    lax.fori_loop(0, live_groups(count), group, 0)


def last_kernel(rows, cols, count, where_at, tiles, u, v, xrt, xc, omega_out, grad_out, obuf, gbuf, zeros, sem):
    live = count[0]
    groups, total = live_groups(count), omega_out.shape[0] // GROUP

    def writes(g, o, d):
        here = pl.ds(g * GROUP, GROUP)
        return (
            pltpu.make_async_copy(o, omega_out.at[here], sem.at[0, g]),
            pltpu.make_async_copy(d, grad_out.at[here], sem.at[1, g]),
        )

    zeros[...] = jnp.zeros_like(zeros)

    def dead(g, _):
        for copy in writes(g, zeros, zeros):
            copy.start()
        return 0

    lax.fori_loop(groups, total, dead, 0)

    def group(g, _):
        for j in range(GROUP):
            k = g * GROUP + j
            grad = gradient(k, live, rows, cols, u, v, xrt, xc)
            gbuf[k] = grad
            obuf[k] = shrunk(jnp.where(k < live, tiles[k], 0.0) - step_size * grad)
        fix_diagonal(g, live, rows, cols, where_at, gbuf, g * GROUP, tiles, obuf)
        here = pl.ds(g * GROUP, GROUP)
        for copy in writes(g, obuf.at[here], gbuf.at[here]):
            copy.start()
        return 0

    lax.fori_loop(0, groups, group, 0)

    def wait(g, _):
        for copy in writes(g, zeros, zeros):
            copy.wait()
        return 0

    lax.fori_loop(0, total, wait, 0)


def tile_call(kernel, scalars, dense, out_shape, out_space, scratch, limit):
    smem = pl.BlockSpec(memory_space=pltpu.SMEM)
    vmem = pl.BlockSpec(memory_space=pltpu.VMEM)
    return pl.pallas_call(
        kernel,
        out_shape=out_shape,
        in_specs=[smem] * 4 + [vmem] * len(dense),
        out_specs=[pl.BlockSpec(memory_space=out_space)] * len(out_shape),
        scratch_shapes=scratch,
        compiler_params=pltpu.CompilerParams(vmem_limit_bytes=limit * MIB),
    )(*scalars, *dense)


def prep(counts, whiten, tiles):
    whiten = lax.dynamic_slice(whiten, (Place().mine // 2, 0, 0), (1, 512, 512)).reshape(512, 512)
    vmem = pl.BlockSpec(memory_space=pltpu.VMEM)
    n = 15 + PARTS * (14 + 7)
    shapes = ((16, 512, 128), (8, 512, 128), (16, 256, 256), (8, 256, 256))
    return pl.pallas_call(
        prep_kernel,
        out_shape=[jax.ShapeDtypeStruct(s, BF16) for s in shapes] + [jax.ShapeDtypeStruct(tiles.shape, F32)],
        in_specs=[pl.BlockSpec(memory_space=pltpu.HBM)] * 2 + [vmem],
        out_specs=[vmem] * 5,
        scratch_shapes=[
            pltpu.VMEM((16, 4096), jnp.int32),
            pltpu.VMEM((8, 16, 512), jnp.int16),
            pltpu.VMEM((16, 16, 512), jnp.int16),
            pltpu.SemaphoreType.DMA((2,)),
            pltpu.SemaphoreType.DMA((2,)),
            pltpu.SemaphoreType.DMA((n,)),
            pltpu.SemaphoreType.DMA((n,)),
        ],
        compiler_params=pltpu.CompilerParams(collective_id=0, has_side_effects=True, vmem_limit_bytes=PREP_MIB * MIB),
    )(counts, tiles, whiten)


def reduce_both(rp, cp, collective_id):
    vmem = pl.BlockSpec(memory_space=pltpu.VMEM)
    n = PARTS * (8 + 7 + 7 + 15 + 7)
    u, v = pl.pallas_call(
        reduce_kernel,
        out_shape=[jax.ShapeDtypeStruct((16, 256, 256), BF16), jax.ShapeDtypeStruct((8, 512, 128), BF16)],
        in_specs=[vmem] * 2,
        out_specs=[vmem] * 2,
        scratch_shapes=[
            pltpu.VMEM((16, 256, 256), BF16),
            pltpu.VMEM((8, 512, 128), BF16),
            pltpu.VMEM((8, 256, 256), BF16),
            pltpu.VMEM((8, 256, 256), BF16),
            pltpu.VMEM((6, 256, 256), BF16),
            pltpu.VMEM((2, 256, 256), BF16),
            pltpu.VMEM((256, 256), F32),
            pltpu.VMEM((6, 512, 128), BF16),
            pltpu.VMEM((2, 512, 128), BF16),
            pltpu.VMEM((512, 128), F32),
            pltpu.SemaphoreType.DMA((n,)),
            pltpu.SemaphoreType.DMA((n,)),
        ],
        compiler_params=pltpu.CompilerParams(
            collective_id=collective_id, has_side_effects=True, vmem_limit_bytes=12 * MIB
        ),
    )(rp.reshape(16, 256, 256), cp.reshape(8, 512, 128))
    return u.reshape(32, 128, 256), v.reshape(16, 256, 128)


def local(counts, whiten, initial_tiles, tile_rows, tile_cols, tile_count):
    where_at = jnp.stack([lax.axis_index("row") * 32, lax.axis_index("col") * 16]).astype(jnp.int32)
    scalars = (tile_rows.reshape(96), tile_cols.reshape(96), tile_count.reshape(1), where_at)
    xr, xc, xrt, xct, tiles = prep(counts, whiten, initial_tiles.reshape(96, 128, 128))
    xr, xc = xr.reshape(32, 256, 128), xc.reshape(16, 256, 128)
    xrt, xct = xrt.reshape(32, 128, 256), xct.reshape(16, 128, 256)
    omega_shape = jax.ShapeDtypeStruct(tiles.shape, F32)
    part_shapes = [jax.ShapeDtypeStruct((32, 128, 256), F32), jax.ShapeDtypeStruct((16, 256, 128), F32)]
    rp, cp = tile_call(first_kernel, scalars, (tiles, xr, xct), part_shapes, pltpu.VMEM, [], 10)
    u, v = reduce_both(rp, cp, 1)
    omega, rp, cp = tile_call(
        middle_kernel, scalars, (tiles, u, v, xrt, xc, xr, xct), [omega_shape] + part_shapes, pltpu.VMEM,
        [pltpu.VMEM((GROUP, 128, 128), F32)], 10,
    )
    u, v = reduce_both(rp, cp, 2)
    buffers = [pltpu.VMEM(tiles.shape, F32)] * 2 + [pltpu.VMEM((GROUP, 128, 128), F32)]
    omega, grad = tile_call(
        last_kernel, scalars, (omega, u, v, xrt, xc), [omega_shape] * 2, pltpu.HBM,
        buffers + [pltpu.SemaphoreType.DMA((2, 96 // GROUP))], 20,
    )
    return omega.reshape(initial_tiles.shape), grad.reshape(initial_tiles.shape)


def solution(mesh):
    in_specs = (
        P("col", "row"),
        P("row", None, None),
        P("row", "col", None, None, None),
        P("row", "col", None),
        P("row", "col", None),
        P("row", "col"),
    )
    out_specs = (P("row", "col", None, None, None), P("row", "col", None, None, None))
    return jax.shard_map(local, mesh=mesh, in_specs=in_specs, out_specs=out_specs, check_vma=False)
```

```python
import functools

import jax
import jax.numpy as jnp
from jax import lax
from jax.experimental import pallas as pl
from jax.experimental.pallas import tpu as pltpu
from jax.sharding import PartitionSpec as P

step_size = 0.08
penalty = 1.0
epsilon = 1e-05
MESH = pl.DeviceIdType.MESH
F32 = jnp.float32
BF16 = jnp.bfloat16
GROUP = 24
MIB = 2**20
PREP_MIB = 41


class Place:
    def __init__(self):
        self.row = lax.axis_index("row")
        self.col = lax.axis_index("col")
        self.y, self.zh = self.row // 2, self.row % 2
        self.zl, self.x, self.core = self.col // 8, (self.col // 2) % 4, self.col % 2
        self.mine = self.core * 8 + self.x * 2 + self.zl
        self.mine_col = self.row

    def at(self, row=None, col=None):
        return (self.row if row is None else row, self.col if col is None else col)

    def xpeer(self, d):
        return self.at(col=self.zl * 8 + ((self.x + d) % 4) * 2 + self.core)

    def ypeer(self, d):
        return self.at(row=((self.y + d) % 4) * 2 + self.zh)

    def zlpeer(self):
        return self.at(col=(1 - self.zl) * 8 + self.x * 2 + self.core)

    def zhpeer(self):
        return self.at(row=self.y * 2 + 1 - self.zh)

    def sibling(self):
        return self.at(col=self.zl * 8 + self.x * 2 + 1 - self.core)


class Wire:
    def __init__(self, send_sem, recv_sem):
        self.send_sem, self.recv_sem = send_sem, recv_sem
        self.copies = {}

    def send(self, name, src, dst, device):
        i = len(self.copies)
        copy = pltpu.make_async_remote_copy(
            src_ref=src, dst_ref=dst, send_sem=self.send_sem.at[i],
            recv_sem=self.recv_sem.at[i], device_id=device, device_id_type=MESH,
        )
        copy.start()
        self.copies[name] = copy

    def recv(self, *names):
        for name in names:
            self.copies[name].wait_recv()

    def drain(self):
        for copy in self.copies.values():
            copy.wait_send()


class Stream:
    def __init__(self, part, parts):
        self.part, self.parts = part, parts

    def rows(self, ref):
        size = ref.shape[-2] // self.parts
        return pl.ds(self.part * size, size)

    def cut(self, ref, i):
        return ref.at[i, self.rows(ref)]


class Gather:
    def __init__(self, wire, stream, tag, out, base, position, z, ring, sibling, done, relayed):
        self.w, self.stream, self.tag, self.out = wire, stream, f"{tag}{stream.part}", out
        self.base, self.position, self.z = base, position, z
        self.ring, self.sibling, self.done, self.relayed = ring, sibling, done, relayed
        self.shared = []

    def slot(self, d, other):
        z = 1 - self.z if other else self.z
        return self.base + ((self.position + d) % 4) * 2 + z

    def pass_on(self, name, slot, device):
        part = self.stream.cut(self.out, slot)
        self.w.send(f"{self.tag}{name}", part, part, device)

    def have(self, d, other):
        s = self.slot(d, other)
        if self.sibling is not None:
            self.pass_on(f"core{d}{other}", s, self.sibling)
            self.shared.append((d, other))
        self.done(s)

    def exchange(self, zpeer):
        self.pass_on("z", self.slot(0, 0), zpeer)

    def exchanged(self):
        self.w.recv(self.tag + "z")

    def start(self, other):
        for d in (1, 3) if self.relayed else (1, 3, 2):
            self.pass_on(f"{other}{d}", self.slot(0, other), self.ring(d))
        self.have(0, other)

    def arrive(self, other, d):
        self.w.recv(f"{self.tag}{other}{d}")
        if self.relayed and (other, d) in ((0, 1), (1, 3)):
            self.pass_on(f"{other}2", self.slot(4 - d, other), self.ring(d))
        self.have(4 - d, other)

    def rest(self):
        for d, other in self.shared:
            self.w.recv(f"{self.tag}core{d}{other}")
            self.done(self.slot(d, other) + 8 - 2 * self.base)


def arrivals(gathers):
    for other in (0, 1):
        for d in (1, 3, 2):
            for gather in gathers:
                gather.arrive(other, d)
    for gather in gathers:
        gather.rest()


def row_gather(wire, stream, place, out, done, relayed):
    return Gather(
        wire, stream, "r", out, place.core * 8, place.x, place.zl, place.xpeer, place.sibling(), done, relayed
    )


def col_gather(wire, stream, place, out, done, relayed):
    return Gather(wire, stream, "c", out, 0, place.y, place.zh, place.ypeer, None, done, relayed)


PARTS = 2


def greet(devices):
    barrier = pltpu.get_barrier_semaphore()
    for device in devices:
        pl.semaphore_signal(barrier, inc=1, device_id=device, device_id_type=MESH)
    return barrier


def prep_kernel(
    counts_hbm, tiles_hbm, whiten, xc, xrt, xct, tiles, xr, counts, packed, landed, wsem, lsem, send_sem, recv_sem
):
    place = Place()
    block = place.mine // 2
    to_row, to_col = place.x * 2 + place.zl, 2 * place.row + place.core
    from_row, from_col = place.col // 2, (place.row % 2) * 8 + (place.row // 2) * 2 + place.core
    moves = jnp.logical_or(to_row != place.row, to_col != place.col)
    peers = [place.at(col=(place.col + d) % 16) for d in range(1, 16)]
    peers += [place.ypeer(d) for d in (1, 2, 3)] + [place.zhpeer()]
    barrier = greet(peers)

    @pl.when(moves)
    def _():
        for device in ((to_row, to_col), (from_row, from_col)):
            pl.semaphore_signal(barrier, inc=1, device_id=device, device_id_type=MESH)

    counted = pltpu.make_async_copy(counts_hbm, counts, wsem.at[0])
    tiled = pltpu.make_async_copy(tiles_hbm, tiles, wsem.at[1])
    counted.start()
    tiled.start()
    counted.wait()
    for b in range(8):
        packed[b] = counts[:, b * 512 : (b + 1) * 512].astype(jnp.int16)
    pl.semaphore_wait(barrier, len(peers) + 2 * moves.astype(jnp.int32))

    wire = Wire(send_sem, recv_sem)
    for d in range(1, 16):
        c = (place.col + d) % 16
        b = (c % 2) * 4 + (c // 2) % 4
        wire.send(f"a{d}", packed.at[b], landed.at[place.col], place.at(col=c))
    landed[place.col] = packed[block]
    wire.recv(*[f"a{d}" for d in range(1, 16)])
    logged = jnp.log(1.0 + landed[...].astype(jnp.int32).astype(F32)).reshape(256, 512)
    mean = jnp.mean(logged, axis=0, keepdims=True)
    centered = logged - mean
    variance = jnp.mean(centered * centered, axis=0, keepdims=True)
    standard = (centered * lax.rsqrt(variance + epsilon)).astype(BF16)
    whitened = jnp.dot(standard, whiten[...], preferred_element_type=F32).astype(BF16)
    pair = block * 2
    for j in range(4):
        xr[pair + j // 2, j % 2 * 256 : (j % 2 + 1) * 256] = whitened[:, j * 128 : (j + 1) * 128]

    def turn(source, target, part):
        def done(s):
            for t in range(2 // PARTS * part, 2 // PARTS * (part + 1)):
                target[s, t * 128 : (t + 1) * 128] = source[s, t * 256 : (t + 1) * 256].T

        return done

    streams = [Stream(p, PARTS) for p in range(PARTS)]
    rows = [row_gather(wire, t, place, xr, turn(xr, xrt, t.part), True) for t in streams]
    cols = [col_gather(wire, t, place, xc, turn(xc, xct, t.part), True) for t in streams]
    hop = pltpu.make_async_remote_copy(
        src_ref=xr.at[place.mine], dst_ref=xc.at[to_row], send_sem=lsem.at[0],
        recv_sem=lsem.at[1], device_id=(to_row, to_col), device_id_type=MESH,
    )

    @pl.when(moves)
    def _():
        hop.start()

    @pl.when(jnp.logical_not(moves))
    def _():
        xc[place.mine_col] = xr[place.mine]

    for row in rows:
        row.start(0)
        row.start(1)

    @pl.when(moves)
    def _():
        hop.wait_recv()

    for col in cols:
        col.exchange(place.zhpeer())
        col.start(0)
    for row in rows:
        row.arrive(0, 1)
        row.arrive(1, 3)
    for col in cols:
        col.arrive(0, 1)
        col.exchanged()
        col.start(1)
    for col in cols:
        col.arrive(0, 3)
    for other, d in ((0, 3), (1, 1), (0, 2), (1, 2)):
        for row in rows:
            row.arrive(other, d)
    for other, d in ((1, 3), (1, 1), (0, 2), (1, 2)):
        for col in cols:
            col.arrive(other, d)
    for row in rows:
        row.rest()
    tiled.wait()
    wire.drain()

    @pl.when(moves)
    def _():
        hop.wait_send()


def add(*parts):
    total = parts[0].astype(F32)
    for part in parts[1:]:
        total = total + part.astype(F32)
    return total


class Scatter:
    def __init__(self, wire, stream, tag, terms, slot, land, ztemp, keep, z, ring, zpeer):
        self.w, self.stream, self.tag = wire, stream, f"{tag}{stream.part}"
        self.terms, self.slot, self.land, self.ztemp, self.keep = terms, slot, land, ztemp, keep
        self.z, self.ring, self.zpeer = z, ring, zpeer

    def term(self, d, e):
        return self.stream.cut(self.terms, self.slot(d, e))

    def landed(self, i):
        return self.stream.cut(self.land, i)

    def put(self, name, i, src, device):
        self.w.send(self.tag + name, src, self.landed(i), device)

    def first(self):
        self.put("A1", 0, self.term(2, 0), self.ring(1))
        self.put("B1", 1, self.term(2, 1), self.ring(3))

    def second(self):
        self.put("A2", 2, self.term(1, 1), self.ring(1))
        self.put("B2", 3, self.term(3, 0), self.ring(3))

    def merge(self):
        for name, i, d, e, then in (("A1", 0, 1, 0, "A3"), ("B1", 1, 3, 1, "B3")):
            self.w.recv(self.tag + name)
            here = self.landed(i)
            here[...] = add(self.term(d, e)[...], here[...]).astype(BF16)
            self.put(then, 4 + i, here, self.ring(d))

    def cross(self):
        self.w.recv(*[self.tag + n for n in ("B2", "A2", "A3", "B3")])
        own = [
            add(self.term(0, e)[...], self.landed(i)[...], self.landed(j)[...]) for e, i, j in ((0, 3, 4), (1, 2, 5))
        ]
        mine = self.z == 0
        out = self.stream.cut(self.ztemp, 0)
        out[...] = jnp.where(mine, own[1], own[0]).astype(BF16)
        self.w.send(self.tag + "Z", out, self.stream.cut(self.ztemp, 1), self.zpeer)
        self.keep[self.stream.rows(self.keep)] = jnp.where(mine, own[0], own[1])

    def last(self, out, slot, turned):
        self.w.recv(self.tag + "Z")
        got = self.stream.cut(self.ztemp, 1)[...]
        total = add(self.keep[self.stream.rows(self.keep)], got).astype(BF16)
        self.stream.cut(out, slot)[...] = total.T if turned else total


def reduce_kernel(rfull, cfull, u, v, rp, cp, pair, summed, rland, rtemp, rkeep, cland, ctemp, ckeep, send_sem, recv_sem):
    place = Place()
    peers = [place.sibling(), place.zlpeer(), place.zhpeer()]
    peers += [place.xpeer(d) for d in (1, 2, 3)] + [place.ypeer(d) for d in (1, 2, 3)]
    barrier = greet(peers)
    rp[...] = rfull[...].astype(BF16)
    cp[...] = cfull[...].astype(BF16)
    pl.semaphore_wait(barrier, len(peers))
    wire = Wire(send_sem, recv_sem)
    here, there = place.core * 8, 8 - place.core * 8

    def rslot(d, e):
        return ((place.x + d) % 4) * 2 + e

    def cslot(d, e):
        return ((place.y + d) % 4) * 2 + e

    streams = [Stream(p, PARTS) for p in range(PARTS)]
    cols = [
        Scatter(wire, t, "cs", cp, cslot, cland, ctemp, ckeep, place.zh, place.ypeer, place.zhpeer()) for t in streams
    ]
    rows = [
        Scatter(wire, t, "rs", summed, rslot, rland, rtemp, rkeep, place.zl, place.xpeer, place.zlpeer())
        for t in streams
    ]
    order = ((2, 0), (2, 1), (1, 1), (3, 0), (1, 0), (3, 1), (0, 0), (0, 1))
    for t in streams:
        for d, e in order:
            s = rslot(d, e)
            wire.send(f"s{t.part}{d}{e}", t.cut(rp, there + s), t.cut(pair, s), place.sibling())
    for col in cols:
        col.first()
        col.second()

    def join(t, which):
        for d, e in which:
            s = rslot(d, e)
            wire.recv(f"s{t.part}{d}{e}")
            t.cut(summed, s)[...] = add(t.cut(rp, here + s)[...], t.cut(pair, s)[...]).astype(BF16)

    for t, row in zip(streams, rows):
        join(t, order[:2])
        row.first()
        join(t, order[2:4])
        row.second()
    for t, row, col in zip(streams, rows, cols):
        col.merge()
        join(t, order[4:6])
        row.merge()
    for t in streams:
        join(t, order[6:])
    for row, col in zip(rows, cols):
        col.cross()
        row.cross()
    nothing = lambda s: None
    rgs = [row_gather(wire, t, place, u, nothing, False) for t in streams]
    cgs = [col_gather(wire, t, place, v, nothing, False) for t in streams]
    for row, col, rg, cg in zip(rows, cols, rgs, cgs):
        col.last(v, place.mine_col, True)
        cg.exchange(place.zhpeer())
        cg.start(0)
        row.last(u, place.mine, False)
        rg.exchange(place.zlpeer())
        rg.start(0)
    for rg, cg in zip(rgs, cgs):
        cg.exchanged()
        cg.start(1)
        rg.exchanged()
        rg.start(1)
    arrivals(cgs + rgs)
    wire.drain()


def live_groups(count):
    return (count[0] + GROUP - 1) // GROUP


def gradient(k, live, rows, cols, u, v, xrt, xc):
    sr, sc = rows[k], cols[k]
    left = jnp.dot(u[sr], xc[sc], preferred_element_type=F32)
    right = jnp.dot(xrt[sr], v[sc], preferred_element_type=F32)
    return jnp.where(k < live, (left + right) * (0.5 / 256), 0.0)


def shrunk(moved):
    t = step_size * penalty
    return moved - jnp.clip(moved, -t, t)


def fix_diagonal(g, live, rows, cols, where_at, grads, base, tiles, omega_out):
    for j in range(GROUP):
        k = g * GROUP + j

        @pl.when(jnp.logical_and(k < live, where_at[0] + rows[k] == where_at[1] + cols[k]))
        def _():
            moved = tiles[k] - step_size * grads[base + j]
            diagonal = 0.5 * (moved + jnp.sqrt(moved * moved + 4.0 * step_size))
            row = lax.broadcasted_iota(jnp.int32, (128, 128), 0)
            col = lax.broadcasted_iota(jnp.int32, (128, 128), 1)
            omega_out[k] = jnp.where(row == col, diagonal, omega_out[k])


def products(k, low, rows, cols, xrt, xct, rp, cp):
    sr, sc = rows[k], cols[k]
    rp[sr] += jnp.dot(low, xct[sc], preferred_element_type=F32)
    cp[sc] += jnp.dot(low.T, xrt[sr], preferred_element_type=F32)


def first_kernel(rows, cols, count, where_at, tiles, xrt, xct, rp, cp):
    rp[...] = jnp.zeros_like(rp)
    cp[...] = jnp.zeros_like(cp)
    live = count[0]

    def group(g, _):
        for j in range(GROUP):
            k = g * GROUP + j
            low = jnp.where(k < live, tiles[k], 0.0).astype(BF16)
            products(k, low, rows, cols, xrt, xct, rp, cp)
        return 0

    lax.fori_loop(0, live_groups(count), group, 0)


def middle_kernel(rows, cols, count, where_at, tiles, u, v, xrt, xc, xct, omega_out, rp, cp, grads):
    rp[...] = jnp.zeros_like(rp)
    cp[...] = jnp.zeros_like(cp)
    live = count[0]

    def group(g, _):
        for j in range(GROUP):
            k = g * GROUP + j
            grad = gradient(k, live, rows, cols, u, v, xrt, xc)
            grads[j] = grad
            omega_out[k] = shrunk(jnp.where(k < live, tiles[k], 0.0) - step_size * grad)
        fix_diagonal(g, live, rows, cols, where_at, grads, 0, tiles, omega_out)
        for j in range(GROUP):
            k = g * GROUP + j
            products(k, omega_out[k].astype(BF16), rows, cols, xrt, xct, rp, cp)
        return 0

    lax.fori_loop(0, live_groups(count), group, 0)


def last_kernel(rows, cols, count, where_at, tiles, u, v, xrt, xc, omega_out, grad_out, obuf, gbuf, zeros, sem):
    live = count[0]
    groups, total = live_groups(count), omega_out.shape[0] // GROUP

    def writes(g, o, d):
        here = pl.ds(g * GROUP, GROUP)
        return (
            pltpu.make_async_copy(o, omega_out.at[here], sem.at[0, g]),
            pltpu.make_async_copy(d, grad_out.at[here], sem.at[1, g]),
        )

    zeros[...] = jnp.zeros_like(zeros)

    def dead(g, _):
        for copy in writes(g, zeros, zeros):
            copy.start()
        return 0

    lax.fori_loop(groups, total, dead, 0)

    def group(g, _):
        for j in range(GROUP):
            k = g * GROUP + j
            grad = gradient(k, live, rows, cols, u, v, xrt, xc)
            gbuf[k] = grad
            obuf[k] = shrunk(jnp.where(k < live, tiles[k], 0.0) - step_size * grad)
        fix_diagonal(g, live, rows, cols, where_at, gbuf, g * GROUP, tiles, obuf)
        here = pl.ds(g * GROUP, GROUP)
        for copy in writes(g, obuf.at[here], gbuf.at[here]):
            copy.start()
        return 0

    lax.fori_loop(0, groups, group, 0)

    def wait(g, _):
        for copy in writes(g, zeros, zeros):
            copy.wait()
        return 0

    lax.fori_loop(0, total, wait, 0)


def tile_call(kernel, scalars, dense, out_shape, out_space, scratch, limit):
    smem = pl.BlockSpec(memory_space=pltpu.SMEM)
    vmem = pl.BlockSpec(memory_space=pltpu.VMEM)
    return pl.pallas_call(
        kernel,
        out_shape=out_shape,
        in_specs=[smem] * 4 + [vmem] * len(dense),
        out_specs=[pl.BlockSpec(memory_space=out_space)] * len(out_shape),
        scratch_shapes=scratch,
        compiler_params=pltpu.CompilerParams(vmem_limit_bytes=limit * MIB),
    )(*scalars, *dense)


def prep(counts, whiten, tiles):
    whiten = lax.dynamic_slice(whiten, (Place().mine // 2, 0, 0), (1, 512, 512)).reshape(512, 512)
    vmem = pl.BlockSpec(memory_space=pltpu.VMEM)
    n = 15 + PARTS * (14 + 7)
    shapes = ((8, 512, 128), (16, 256, 256), (8, 256, 256))
    return pl.pallas_call(
        prep_kernel,
        out_shape=[jax.ShapeDtypeStruct(s, BF16) for s in shapes] + [jax.ShapeDtypeStruct(tiles.shape, F32)],
        in_specs=[pl.BlockSpec(memory_space=pltpu.HBM)] * 2 + [vmem],
        out_specs=[vmem] * 4,
        scratch_shapes=[
            pltpu.VMEM((16, 512, 128), BF16),
            pltpu.VMEM((16, 4096), jnp.int32),
            pltpu.VMEM((8, 16, 512), jnp.int16),
            pltpu.VMEM((16, 16, 512), jnp.int16),
            pltpu.SemaphoreType.DMA((2,)),
            pltpu.SemaphoreType.DMA((2,)),
            pltpu.SemaphoreType.DMA((n,)),
            pltpu.SemaphoreType.DMA((n,)),
        ],
        compiler_params=pltpu.CompilerParams(collective_id=0, has_side_effects=True, vmem_limit_bytes=PREP_MIB * MIB),
    )(counts, tiles, whiten)


def reduce_both(rp, cp, collective_id):
    vmem = pl.BlockSpec(memory_space=pltpu.VMEM)
    n = PARTS * (8 + 7 + 7 + 15 + 7)
    u, v = pl.pallas_call(
        reduce_kernel,
        out_shape=[jax.ShapeDtypeStruct((16, 256, 256), BF16), jax.ShapeDtypeStruct((8, 512, 128), BF16)],
        in_specs=[vmem] * 2,
        out_specs=[vmem] * 2,
        scratch_shapes=[
            pltpu.VMEM((16, 256, 256), BF16),
            pltpu.VMEM((8, 256, 256), BF16),
            pltpu.VMEM((8, 256, 256), BF16),
            pltpu.VMEM((8, 256, 256), BF16),
            pltpu.VMEM((6, 256, 256), BF16),
            pltpu.VMEM((2, 256, 256), BF16),
            pltpu.VMEM((256, 256), F32),
            pltpu.VMEM((6, 256, 256), BF16),
            pltpu.VMEM((2, 256, 256), BF16),
            pltpu.VMEM((256, 256), F32),
            pltpu.SemaphoreType.DMA((n,)),
            pltpu.SemaphoreType.DMA((n,)),
        ],
        compiler_params=pltpu.CompilerParams(
            collective_id=collective_id, has_side_effects=True, vmem_limit_bytes=12 * MIB
        ),
    )(rp.reshape(16, 256, 256), cp.reshape(8, 256, 256))
    return u.reshape(32, 128, 256), v.reshape(16, 256, 128)


def local(counts, whiten, initial_tiles, tile_rows, tile_cols, tile_count):
    where_at = jnp.stack([lax.axis_index("row") * 32, lax.axis_index("col") * 16]).astype(jnp.int32)
    scalars = (tile_rows.reshape(96), tile_cols.reshape(96), tile_count.reshape(1), where_at)
    xc, xrt, xct, tiles = prep(counts, whiten, initial_tiles.reshape(96, 128, 128))
    xc = xc.reshape(16, 256, 128)
    xrt, xct = xrt.reshape(32, 128, 256), xct.reshape(16, 128, 256)
    omega_shape = jax.ShapeDtypeStruct(tiles.shape, F32)
    part_shapes = [jax.ShapeDtypeStruct((n, 128, 256), F32) for n in (32, 16)]
    rp, cp = tile_call(first_kernel, scalars, (tiles, xrt, xct), part_shapes, pltpu.VMEM, [], 10)
    u, v = reduce_both(rp, cp, 1)
    omega, rp, cp = tile_call(
        middle_kernel, scalars, (tiles, u, v, xrt, xc, xct), [omega_shape] + part_shapes, pltpu.VMEM,
        [pltpu.VMEM((GROUP, 128, 128), F32)], 10,
    )
    u, v = reduce_both(rp, cp, 2)
    buffers = [pltpu.VMEM(tiles.shape, F32)] * 2 + [pltpu.VMEM((GROUP, 128, 128), F32)]
    omega, grad = tile_call(
        last_kernel, scalars, (omega, u, v, xrt, xc), [omega_shape] * 2, pltpu.HBM,
        buffers + [pltpu.SemaphoreType.DMA((2, 96 // GROUP))], 20,
    )
    return omega.reshape(initial_tiles.shape), grad.reshape(initial_tiles.shape)


def solution(mesh):
    in_specs = (
        P("col", "row"),
        P("row", None, None),
        P("row", "col", None, None, None),
        P("row", "col", None),
        P("row", "col", None),
        P("row", "col"),
    )
    out_specs = (P("row", "col", None, None, None), P("row", "col", None, None, None))
    return jax.shard_map(local, mesh=mesh, in_specs=in_specs, out_specs=out_specs, check_vma=False)
```

```python
import functools

import jax
import jax.numpy as jnp
from jax import lax
from jax.experimental import pallas as pl
from jax.experimental.pallas import tpu as pltpu
from jax.sharding import PartitionSpec as P

step_size = 0.08
penalty = 1.0
epsilon = 1e-05
MESH = pl.DeviceIdType.MESH
F32 = jnp.float32
BF16 = jnp.bfloat16
GROUP = 24
MIB = 2**20
PREP_MIB = 41


class Place:
    def __init__(self):
        self.row = lax.axis_index("row")
        self.col = lax.axis_index("col")
        self.y, self.zh = self.row // 2, self.row % 2
        self.zl, self.x, self.core = self.col // 8, (self.col // 2) % 4, self.col % 2
        self.mine = self.core * 8 + self.x * 2 + self.zl
        self.mine_col = self.row

    def at(self, row=None, col=None):
        return (self.row if row is None else row, self.col if col is None else col)

    def xpeer(self, d):
        return self.at(col=self.zl * 8 + ((self.x + d) % 4) * 2 + self.core)

    def ypeer(self, d):
        return self.at(row=((self.y + d) % 4) * 2 + self.zh)

    def zlpeer(self):
        return self.at(col=(1 - self.zl) * 8 + self.x * 2 + self.core)

    def zhpeer(self):
        return self.at(row=self.y * 2 + 1 - self.zh)

    def sibling(self):
        return self.at(col=self.zl * 8 + self.x * 2 + 1 - self.core)


class Wire:
    def __init__(self, send_sem, recv_sem):
        self.send_sem, self.recv_sem = send_sem, recv_sem
        self.copies = {}

    def send(self, name, src, dst, device):
        i = len(self.copies)
        copy = pltpu.make_async_remote_copy(
            src_ref=src, dst_ref=dst, send_sem=self.send_sem.at[i],
            recv_sem=self.recv_sem.at[i], device_id=device, device_id_type=MESH,
        )
        copy.start()
        self.copies[name] = copy

    def recv(self, *names):
        for name in names:
            self.copies[name].wait_recv()

    def drain(self):
        for copy in self.copies.values():
            copy.wait_send()


class Stream:
    def __init__(self, part, parts):
        self.part, self.parts = part, parts

    def rows(self, ref):
        size = ref.shape[-2] // self.parts
        return pl.ds(self.part * size, size)

    def cut(self, ref, i):
        return ref.at[i, self.rows(ref)]


class Gather:
    def __init__(self, wire, stream, tag, out, base, position, z, ring, sibling, done, relayed):
        self.w, self.stream, self.tag, self.out = wire, stream, f"{tag}{stream.part}", out
        self.base, self.position, self.z = base, position, z
        self.ring, self.sibling, self.done, self.relayed = ring, sibling, done, relayed
        self.shared = []

    def slot(self, d, other):
        z = 1 - self.z if other else self.z
        return self.base + ((self.position + d) % 4) * 2 + z

    def pass_on(self, name, slot, device):
        part = self.stream.cut(self.out, slot)
        self.w.send(f"{self.tag}{name}", part, part, device)

    def have(self, d, other):
        s = self.slot(d, other)
        if self.sibling is not None:
            self.pass_on(f"core{d}{other}", s, self.sibling)
            self.shared.append((d, other))
        self.done(s)

    def exchange(self, zpeer):
        self.pass_on("z", self.slot(0, 0), zpeer)

    def exchanged(self):
        self.w.recv(self.tag + "z")

    def start(self, other):
        for d in (1, 3) if self.relayed else (1, 3, 2):
            self.pass_on(f"{other}{d}", self.slot(0, other), self.ring(d))
        self.have(0, other)

    def arrive(self, other, d):
        self.w.recv(f"{self.tag}{other}{d}")
        if self.relayed and (other, d) in ((0, 1), (1, 3)):
            self.pass_on(f"{other}2", self.slot(4 - d, other), self.ring(d))
        self.have(4 - d, other)

    def rest(self):
        for d, other in self.shared:
            self.w.recv(f"{self.tag}core{d}{other}")
            self.done(self.slot(d, other) + 8 - 2 * self.base)


def row_gather(wire, stream, place, out, done, relayed):
    return Gather(
        wire, stream, "r", out, place.core * 8, place.x, place.zl, place.xpeer, place.sibling(), done, relayed
    )


def col_gather(wire, stream, place, out, done, relayed):
    return Gather(wire, stream, "c", out, 0, place.y, place.zh, place.ypeer, None, done, relayed)


PARTS = 2


def greet(devices):
    barrier = pltpu.get_barrier_semaphore()
    for device in devices:
        pl.semaphore_signal(barrier, inc=1, device_id=device, device_id_type=MESH)
    return barrier


def prep_kernel(
    counts_hbm, tiles_hbm, whiten, xc, xrt, xct, tiles, xr, counts, packed, landed, wsem, lsem, send_sem, recv_sem
):
    place = Place()
    block = place.mine // 2
    to_row, to_col = place.x * 2 + place.zl, 2 * place.row + place.core
    from_row, from_col = place.col // 2, (place.row % 2) * 8 + (place.row // 2) * 2 + place.core
    moves = jnp.logical_or(to_row != place.row, to_col != place.col)
    peers = [place.at(col=(place.col + d) % 16) for d in range(1, 16)]
    peers += [place.ypeer(d) for d in (1, 2, 3)] + [place.zhpeer()]
    barrier = greet(peers)

    @pl.when(moves)
    def _():
        for device in ((to_row, to_col), (from_row, from_col)):
            pl.semaphore_signal(barrier, inc=1, device_id=device, device_id_type=MESH)

    counted = pltpu.make_async_copy(counts_hbm, counts, wsem.at[0])
    tiled = pltpu.make_async_copy(tiles_hbm, tiles, wsem.at[1])
    counted.start()
    tiled.start()
    counted.wait()
    for b in range(8):
        packed[b] = counts[:, b * 512 : (b + 1) * 512].astype(jnp.int16)
    pl.semaphore_wait(barrier, len(peers) + 2 * moves.astype(jnp.int32))

    wire = Wire(send_sem, recv_sem)
    for d in range(1, 16):
        c = (place.col + d) % 16
        b = (c % 2) * 4 + (c // 2) % 4
        wire.send(f"a{d}", packed.at[b], landed.at[place.col], place.at(col=c))
    landed[place.col] = packed[block]
    wire.recv(*[f"a{d}" for d in range(1, 16)])
    logged = jnp.log(1.0 + landed[...].astype(jnp.int32).astype(F32)).reshape(256, 512)
    mean = jnp.mean(logged, axis=0, keepdims=True)
    centered = logged - mean
    variance = jnp.mean(centered * centered, axis=0, keepdims=True)
    standard = (centered * lax.rsqrt(variance + epsilon)).astype(BF16)
    whitened = jnp.dot(standard, whiten[...], preferred_element_type=F32).astype(BF16)
    pair = block * 2
    for j in range(4):
        xr[pair + j // 2, j % 2 * 256 : (j % 2 + 1) * 256] = whitened[:, j * 128 : (j + 1) * 128]

    def turn(source, target, part):
        def done(s):
            for t in range(2 // PARTS * part, 2 // PARTS * (part + 1)):
                target[s, t * 128 : (t + 1) * 128] = source[s, t * 256 : (t + 1) * 256].T

        return done

    streams = [Stream(p, PARTS) for p in range(PARTS)]
    rows = [row_gather(wire, t, place, xr, turn(xr, xrt, t.part), True) for t in streams]
    cols = [col_gather(wire, t, place, xc, turn(xc, xct, t.part), True) for t in streams]
    hop = pltpu.make_async_remote_copy(
        src_ref=xr.at[place.mine], dst_ref=xc.at[to_row], send_sem=lsem.at[0],
        recv_sem=lsem.at[1], device_id=(to_row, to_col), device_id_type=MESH,
    )

    @pl.when(moves)
    def _():
        hop.start()

    @pl.when(jnp.logical_not(moves))
    def _():
        xc[place.mine_col] = xr[place.mine]

    for row in rows:
        row.start(0)
        row.start(1)

    @pl.when(moves)
    def _():
        hop.wait_recv()

    for col in cols:
        col.exchange(place.zhpeer())
        col.start(0)
    for row in rows:
        row.arrive(0, 1)
        row.arrive(1, 3)
    for col in cols:
        col.arrive(0, 1)
        col.exchanged()
        col.start(1)
    for col in cols:
        col.arrive(0, 3)
    for other, d in ((0, 3), (1, 1), (0, 2), (1, 2)):
        for row in rows:
            row.arrive(other, d)
    for other, d in ((1, 3), (1, 1), (0, 2), (1, 2)):
        for col in cols:
            col.arrive(other, d)
    for row in rows:
        row.rest()
    tiled.wait()
    wire.drain()

    @pl.when(moves)
    def _():
        hop.wait_send()


def add(*parts):
    total = parts[0].astype(F32)
    for part in parts[1:]:
        total = total + part.astype(F32)
    return total


class Scatter:
    def __init__(self, wire, stream, tag, terms, slot, land, ztemp, keep, z, ring, zpeer):
        self.w, self.stream, self.tag = wire, stream, f"{tag}{stream.part}"
        self.terms, self.slot, self.land, self.ztemp, self.keep = terms, slot, land, ztemp, keep
        self.z, self.ring, self.zpeer = z, ring, zpeer

    def term(self, d, e):
        return self.stream.cut(self.terms, self.slot(d, e))

    def landed(self, i):
        return self.stream.cut(self.land, i)

    def put(self, name, i, src, device):
        self.w.send(self.tag + name, src, self.landed(i), device)

    def first(self):
        self.put("A1", 0, self.term(2, 0), self.ring(1))
        self.put("B1", 1, self.term(2, 1), self.ring(3))

    def second(self):
        self.put("A2", 2, self.term(1, 1), self.ring(1))
        self.put("B2", 3, self.term(3, 0), self.ring(3))

    def merge(self):
        for name, i, d, e, then in (("A1", 0, 1, 0, "A3"), ("B1", 1, 3, 1, "B3")):
            self.w.recv(self.tag + name)
            here = self.landed(i)
            here[...] = add(self.term(d, e)[...], here[...]).astype(BF16)
            self.put(then, 4 + i, here, self.ring(d))

    def cross(self):
        self.w.recv(*[self.tag + n for n in ("B2", "A2", "A3", "B3")])
        own = [
            add(self.term(0, e)[...], self.landed(i)[...], self.landed(j)[...]) for e, i, j in ((0, 3, 4), (1, 2, 5))
        ]
        mine = self.z == 0
        out = self.stream.cut(self.ztemp, 0)
        out[...] = jnp.where(mine, own[1], own[0]).astype(BF16)
        self.w.send(self.tag + "Z", out, self.stream.cut(self.ztemp, 1), self.zpeer)
        self.keep[self.stream.rows(self.keep)] = jnp.where(mine, own[0], own[1])

    def last(self, out, slot, turned):
        self.w.recv(self.tag + "Z")
        got = self.stream.cut(self.ztemp, 1)[...]
        total = add(self.keep[self.stream.rows(self.keep)], got).astype(BF16)
        self.stream.cut(out, slot)[...] = total.T if turned else total


class ZFirst:
    def __init__(self, wire, stream, place, summed, slot, zin, sums, xin, keep, out):
        self.w, self.stream, self.place, self.tag = wire, stream, place, f"zf{stream.part}"
        self.summed, self.slot, self.zin, self.sums, self.xin = summed, slot, zin, sums, xin
        self.keep, self.out, self.shared = keep, out, []

    def cross(self, d):
        src = self.stream.cut(self.summed, self.slot(d, 1 - self.place.zl))
        self.w.send(f"{self.tag}z{d}", src, self.stream.cut(self.zin, d), self.place.zlpeer())

    def merge(self, d):
        self.w.recv(f"{self.tag}z{d}")
        mine = self.stream.cut(self.summed, self.slot(d, self.place.zl))[...]
        total = add(mine, self.stream.cut(self.zin, d)[...])
        if d == 0:
            self.keep[self.stream.rows(self.keep)] = total
            return
        out = self.stream.cut(self.sums, d - 1)
        out[...] = total.astype(BF16)
        self.w.send(f"{self.tag}x{d}", out, self.stream.cut(self.xin, d - 1), self.place.xpeer(d))

    def last(self):
        parts = [self.keep[self.stream.rows(self.keep)]]
        for d in (1, 2, 3):
            self.w.recv(f"{self.tag}x{d}")
            parts.append(self.stream.cut(self.xin, d - 1)[...])
        self.stream.cut(self.out, self.place.mine)[...] = add(*parts).astype(BF16)
        for d in (1, 3, 2):
            self.pass_on(f"g{d}", self.at(0, 0), self.place.xpeer(d))
        self.pass_on("c0", self.at(0, 0), self.place.zlpeer())
        self.have(0, 0)

    def at(self, d, other):
        z = 1 - self.place.zl if other else self.place.zl
        return self.place.core * 8 + ((self.place.x + d) % 4) * 2 + z

    def pass_on(self, name, slot, device):
        part = self.stream.cut(self.out, slot)
        self.w.send(self.tag + name, part, part, device)

    def have(self, d, other):
        self.pass_on(f"core{d}{other}", self.at(d, other), self.place.sibling())
        self.shared.append((d, other))

    def near(self, d):
        self.w.recv(f"{self.tag}g{d}")
        self.pass_on(f"c{4 - d}", self.at(4 - d, 0), self.place.zlpeer())
        self.have(4 - d, 0)

    def beyond(self, d):
        self.w.recv(f"{self.tag}c{d}")
        self.have(d, 1)

    def rest(self):
        for d, other in self.shared:
            self.w.recv(f"{self.tag}core{d}{other}")


def reduce_kernel(rfull, cfull, u, v, rp, cp, pair, summed, rland, rtemp, rkeep, zin, sums, xin, cland, ctemp, ckeep, send_sem, recv_sem):
    place = Place()
    peers = [place.sibling(), place.zlpeer(), place.zhpeer()]
    peers += [place.xpeer(d) for d in (1, 2, 3)] + [place.ypeer(d) for d in (1, 2, 3)]
    barrier = greet(peers)
    rp[...] = rfull[...].astype(BF16)
    cp[...] = cfull[...].astype(BF16)
    pl.semaphore_wait(barrier, len(peers))
    wire = Wire(send_sem, recv_sem)
    here, there = place.core * 8, 8 - place.core * 8

    def rslot(d, e):
        return ((place.x + d) % 4) * 2 + e

    def cslot(d, e):
        return ((place.y + d) % 4) * 2 + e

    streams = [Stream(p, PARTS) for p in range(PARTS)]
    cols = [
        Scatter(wire, t, "cs", cp, cslot, cland, ctemp, ckeep, place.zh, place.ypeer, place.zhpeer()) for t in streams
    ]
    row = Scatter(wire, streams[0], "rs", summed, rslot, rland, rtemp, rkeep, place.zl, place.xpeer, place.zlpeer())
    other = ZFirst(wire, streams[1], place, summed, rslot, zin, sums, xin, rkeep, u)
    order = ((2, 0), (2, 1), (1, 1), (3, 0), (1, 0), (3, 1), (0, 0), (0, 1))
    for t in streams:
        for d, e in order:
            s = rslot(d, e)
            wire.send(f"s{t.part}{d}{e}", t.cut(rp, there + s), t.cut(pair, s), place.sibling())
    for col in cols:
        col.first()
        col.second()

    def join(t, which):
        for d, e in which:
            s = rslot(d, e)
            wire.recv(f"s{t.part}{d}{e}")
            t.cut(summed, s)[...] = add(t.cut(rp, here + s)[...], t.cut(pair, s)[...]).astype(BF16)

    one, two = streams
    join(one, order[:2])
    row.first()
    join(two, order[:2])
    other.cross(2)
    join(one, order[2:4])
    row.second()
    join(two, order[2:6])
    other.cross(1)
    other.cross(3)
    join(two, order[6:])
    other.cross(0)
    cols[0].merge()
    join(one, order[4:6])
    row.merge()
    other.merge(2)
    cols[1].merge()
    other.merge(1)
    other.merge(3)
    join(one, order[6:])
    cols[0].cross()
    row.cross()
    other.merge(0)
    cols[1].cross()
    nothing = lambda s: None
    rg = row_gather(wire, one, place, u, nothing, False)
    cgs = [col_gather(wire, t, place, v, nothing, False) for t in streams]
    for i in range(2):
        cols[i].last(v, place.mine_col, True)
        cgs[i].exchange(place.zhpeer())
        cgs[i].start(0)
        if i == 0:
            row.last(u, place.mine, False)
            rg.exchange(place.zlpeer())
            rg.start(0)
        else:
            other.last()
    for d in (1, 3, 2):
        cgs[0].arrive(0, d)
        rg.arrive(0, d)
    for g in (cgs[0], rg, cgs[1]):
        g.exchanged()
        g.start(1)
    for d in (1, 3, 2):
        other.near(d)
        cgs[1].arrive(0, d)
    other.beyond(0)
    for d in (1, 3, 2):
        cgs[0].arrive(1, d)
        rg.arrive(1, d)
    for d in (3, 1, 2):
        other.beyond(d)
        cgs[1].arrive(1, d)
    rg.rest()
    other.rest()
    wire.drain()


def live_groups(count):
    return (count[0] + GROUP - 1) // GROUP


def gradient(k, live, rows, cols, u, v, xrt, xc):
    sr, sc = rows[k], cols[k]
    left = jnp.dot(u[sr], xc[sc], preferred_element_type=F32)
    right = jnp.dot(xrt[sr], v[sc], preferred_element_type=F32)
    return jnp.where(k < live, (left + right) * (0.5 / 256), 0.0)


def shrunk(moved):
    t = step_size * penalty
    return moved - jnp.clip(moved, -t, t)


def fix_diagonal(g, live, rows, cols, where_at, grads, base, tiles, omega_out):
    for j in range(GROUP):
        k = g * GROUP + j

        @pl.when(jnp.logical_and(k < live, where_at[0] + rows[k] == where_at[1] + cols[k]))
        def _():
            moved = tiles[k] - step_size * grads[base + j]
            diagonal = 0.5 * (moved + jnp.sqrt(moved * moved + 4.0 * step_size))
            row = lax.broadcasted_iota(jnp.int32, (128, 128), 0)
            col = lax.broadcasted_iota(jnp.int32, (128, 128), 1)
            omega_out[k] = jnp.where(row == col, diagonal, omega_out[k])


def products(k, low, rows, cols, xrt, xct, rp, cp):
    sr, sc = rows[k], cols[k]
    rp[sr] += jnp.dot(low, xct[sc], preferred_element_type=F32)
    cp[sc] += jnp.dot(low.T, xrt[sr], preferred_element_type=F32)


def first_kernel(rows, cols, count, where_at, tiles, xrt, xct, rp, cp):
    rp[...] = jnp.zeros_like(rp)
    cp[...] = jnp.zeros_like(cp)
    live = count[0]

    def group(g, _):
        for j in range(GROUP):
            k = g * GROUP + j
            low = jnp.where(k < live, tiles[k], 0.0).astype(BF16)
            products(k, low, rows, cols, xrt, xct, rp, cp)
        return 0

    lax.fori_loop(0, live_groups(count), group, 0)


def middle_kernel(rows, cols, count, where_at, tiles, u, v, xrt, xc, xct, omega_out, rp, cp, grads):
    rp[...] = jnp.zeros_like(rp)
    cp[...] = jnp.zeros_like(cp)
    live = count[0]

    def group(g, _):
        for j in range(GROUP):
            k = g * GROUP + j
            grad = gradient(k, live, rows, cols, u, v, xrt, xc)
            grads[j] = grad
            omega_out[k] = shrunk(jnp.where(k < live, tiles[k], 0.0) - step_size * grad)
        fix_diagonal(g, live, rows, cols, where_at, grads, 0, tiles, omega_out)
        for j in range(GROUP):
            k = g * GROUP + j
            products(k, omega_out[k].astype(BF16), rows, cols, xrt, xct, rp, cp)
        return 0

    lax.fori_loop(0, live_groups(count), group, 0)


def last_kernel(rows, cols, count, where_at, tiles, u, v, xrt, xc, omega_out, grad_out, obuf, gbuf, zeros, sem):
    live = count[0]
    groups, total = live_groups(count), omega_out.shape[0] // GROUP

    def writes(g, o, d):
        here = pl.ds(g * GROUP, GROUP)
        return (
            pltpu.make_async_copy(o, omega_out.at[here], sem.at[0, g]),
            pltpu.make_async_copy(d, grad_out.at[here], sem.at[1, g]),
        )

    zeros[...] = jnp.zeros_like(zeros)

    def dead(g, _):
        for copy in writes(g, zeros, zeros):
            copy.start()
        return 0

    lax.fori_loop(groups, total, dead, 0)

    def group(g, _):
        for j in range(GROUP):
            k = g * GROUP + j
            grad = gradient(k, live, rows, cols, u, v, xrt, xc)
            gbuf[k] = grad
            obuf[k] = shrunk(jnp.where(k < live, tiles[k], 0.0) - step_size * grad)
        fix_diagonal(g, live, rows, cols, where_at, gbuf, g * GROUP, tiles, obuf)
        here = pl.ds(g * GROUP, GROUP)
        for copy in writes(g, obuf.at[here], gbuf.at[here]):
            copy.start()
        return 0

    lax.fori_loop(0, groups, group, 0)

    def wait(g, _):
        for copy in writes(g, zeros, zeros):
            copy.wait()
        return 0

    lax.fori_loop(0, total, wait, 0)


def tile_call(kernel, scalars, dense, out_shape, out_space, scratch, limit):
    smem = pl.BlockSpec(memory_space=pltpu.SMEM)
    vmem = pl.BlockSpec(memory_space=pltpu.VMEM)
    return pl.pallas_call(
        kernel,
        out_shape=out_shape,
        in_specs=[smem] * 4 + [vmem] * len(dense),
        out_specs=[pl.BlockSpec(memory_space=out_space)] * len(out_shape),
        scratch_shapes=scratch,
        compiler_params=pltpu.CompilerParams(vmem_limit_bytes=limit * MIB),
    )(*scalars, *dense)


def prep(counts, whiten, tiles):
    whiten = lax.dynamic_slice(whiten, (Place().mine // 2, 0, 0), (1, 512, 512)).reshape(512, 512)
    vmem = pl.BlockSpec(memory_space=pltpu.VMEM)
    n = 15 + PARTS * (14 + 7)
    shapes = ((8, 512, 128), (16, 256, 256), (8, 256, 256))
    return pl.pallas_call(
        prep_kernel,
        out_shape=[jax.ShapeDtypeStruct(s, BF16) for s in shapes] + [jax.ShapeDtypeStruct(tiles.shape, F32)],
        in_specs=[pl.BlockSpec(memory_space=pltpu.HBM)] * 2 + [vmem],
        out_specs=[vmem] * 4,
        scratch_shapes=[
            pltpu.VMEM((16, 512, 128), BF16),
            pltpu.VMEM((16, 4096), jnp.int32),
            pltpu.VMEM((8, 16, 512), jnp.int16),
            pltpu.VMEM((16, 16, 512), jnp.int16),
            pltpu.SemaphoreType.DMA((2,)),
            pltpu.SemaphoreType.DMA((2,)),
            pltpu.SemaphoreType.DMA((n,)),
            pltpu.SemaphoreType.DMA((n,)),
        ],
        compiler_params=pltpu.CompilerParams(collective_id=0, has_side_effects=True, vmem_limit_bytes=PREP_MIB * MIB),
    )(counts, tiles, whiten)


def reduce_both(rp, cp, collective_id):
    vmem = pl.BlockSpec(memory_space=pltpu.VMEM)
    n = PARTS * (8 + 7 + 7 + 15 + 7)
    u, v = pl.pallas_call(
        reduce_kernel,
        out_shape=[jax.ShapeDtypeStruct((16, 256, 256), BF16), jax.ShapeDtypeStruct((8, 512, 128), BF16)],
        in_specs=[vmem] * 2,
        out_specs=[vmem] * 2,
        scratch_shapes=[
            pltpu.VMEM((16, 256, 256), BF16),
            pltpu.VMEM((8, 256, 256), BF16),
            pltpu.VMEM((8, 256, 256), BF16),
            pltpu.VMEM((8, 256, 256), BF16),
            pltpu.VMEM((6, 256, 256), BF16),
            pltpu.VMEM((2, 256, 256), BF16),
            pltpu.VMEM((256, 256), F32),
            pltpu.VMEM((4, 256, 256), BF16),
            pltpu.VMEM((3, 256, 256), BF16),
            pltpu.VMEM((3, 256, 256), BF16),
            pltpu.VMEM((6, 256, 256), BF16),
            pltpu.VMEM((2, 256, 256), BF16),
            pltpu.VMEM((256, 256), F32),
            pltpu.SemaphoreType.DMA((n,)),
            pltpu.SemaphoreType.DMA((n,)),
        ],
        compiler_params=pltpu.CompilerParams(
            collective_id=collective_id, has_side_effects=True, vmem_limit_bytes=12 * MIB
        ),
    )(rp.reshape(16, 256, 256), cp.reshape(8, 256, 256))
    return u.reshape(32, 128, 256), v.reshape(16, 256, 128)


def local(counts, whiten, initial_tiles, tile_rows, tile_cols, tile_count):
    where_at = jnp.stack([lax.axis_index("row") * 32, lax.axis_index("col") * 16]).astype(jnp.int32)
    scalars = (tile_rows.reshape(96), tile_cols.reshape(96), tile_count.reshape(1), where_at)
    xc, xrt, xct, tiles = prep(counts, whiten, initial_tiles.reshape(96, 128, 128))
    xc = xc.reshape(16, 256, 128)
    xrt, xct = xrt.reshape(32, 128, 256), xct.reshape(16, 128, 256)
    omega_shape = jax.ShapeDtypeStruct(tiles.shape, F32)
    part_shapes = [jax.ShapeDtypeStruct((n, 128, 256), F32) for n in (32, 16)]
    rp, cp = tile_call(first_kernel, scalars, (tiles, xrt, xct), part_shapes, pltpu.VMEM, [], 10)
    u, v = reduce_both(rp, cp, 1)
    omega, rp, cp = tile_call(
        middle_kernel, scalars, (tiles, u, v, xrt, xc, xct), [omega_shape] + part_shapes, pltpu.VMEM,
        [pltpu.VMEM((GROUP, 128, 128), F32)], 10,
    )
    u, v = reduce_both(rp, cp, 2)
    buffers = [pltpu.VMEM(tiles.shape, F32)] * 2 + [pltpu.VMEM((GROUP, 128, 128), F32)]
    omega, grad = tile_call(
        last_kernel, scalars, (omega, u, v, xrt, xc), [omega_shape] * 2, pltpu.HBM,
        buffers + [pltpu.SemaphoreType.DMA((2, 96 // GROUP))], 20,
    )
    return omega.reshape(initial_tiles.shape), grad.reshape(initial_tiles.shape)


def solution(mesh):
    in_specs = (
        P("col", "row"),
        P("row", None, None),
        P("row", "col", None, None, None),
        P("row", "col", None),
        P("row", "col", None),
        P("row", "col"),
    )
    out_specs = (P("row", "col", None, None, None), P("row", "col", None, None, None))
    return jax.shard_map(local, mesh=mesh, in_specs=in_specs, out_specs=out_specs, check_vma=False)
```

```python
import functools

import jax
import jax.numpy as jnp
from jax import lax
from jax.experimental import pallas as pl
from jax.experimental.pallas import tpu as pltpu
from jax.sharding import PartitionSpec as P

step_size = 0.08
penalty = 1.0
epsilon = 1e-05
MESH = pl.DeviceIdType.MESH
F32 = jnp.float32
BF16 = jnp.bfloat16
GROUP = 24
MIB = 2**20
PREP_MIB = 41


class Place:
    def __init__(self):
        self.row = lax.axis_index("row")
        self.col = lax.axis_index("col")
        self.y, self.zh = self.row // 2, self.row % 2
        self.zl, self.x, self.core = self.col // 8, (self.col // 2) % 4, self.col % 2
        self.mine = self.core * 8 + self.x * 2 + self.zl
        self.mine_col = self.row

    def at(self, row=None, col=None):
        return (self.row if row is None else row, self.col if col is None else col)

    def xpeer(self, d):
        return self.at(col=self.zl * 8 + ((self.x + d) % 4) * 2 + self.core)

    def ypeer(self, d):
        return self.at(row=((self.y + d) % 4) * 2 + self.zh)

    def zlpeer(self):
        return self.at(col=(1 - self.zl) * 8 + self.x * 2 + self.core)

    def zhpeer(self):
        return self.at(row=self.y * 2 + 1 - self.zh)

    def sibling(self):
        return self.at(col=self.zl * 8 + self.x * 2 + 1 - self.core)


class Wire:
    def __init__(self, send_sem, recv_sem):
        self.send_sem, self.recv_sem = send_sem, recv_sem
        self.copies = {}

    def send(self, name, src, dst, device):
        i = len(self.copies)
        copy = pltpu.make_async_remote_copy(
            src_ref=src, dst_ref=dst, send_sem=self.send_sem.at[i],
            recv_sem=self.recv_sem.at[i], device_id=device, device_id_type=MESH,
        )
        copy.start()
        self.copies[name] = copy

    def recv(self, *names):
        for name in names:
            self.copies[name].wait_recv()

    def drain(self):
        for copy in self.copies.values():
            copy.wait_send()


class Stream:
    def __init__(self, part, parts):
        self.part, self.parts = part, parts

    def rows(self, ref):
        size = ref.shape[-2] // self.parts
        return pl.ds(self.part * size, size)

    def cut(self, ref, i):
        return ref.at[i, self.rows(ref)]


class Gather:
    def __init__(self, wire, stream, tag, out, base, position, z, ring, sibling, done, relayed):
        self.w, self.stream, self.tag, self.out = wire, stream, f"{tag}{stream.part}", out
        self.base, self.position, self.z = base, position, z
        self.ring, self.sibling, self.done, self.relayed = ring, sibling, done, relayed
        self.shared = []

    def slot(self, d, other):
        z = 1 - self.z if other else self.z
        return self.base + ((self.position + d) % 4) * 2 + z

    def pass_on(self, name, slot, device):
        part = self.stream.cut(self.out, slot)
        self.w.send(f"{self.tag}{name}", part, part, device)

    def have(self, d, other):
        s = self.slot(d, other)
        if self.sibling is not None:
            self.pass_on(f"core{d}{other}", s, self.sibling)
            self.shared.append((d, other))
        self.done(s)

    def exchange(self, zpeer):
        self.pass_on("z", self.slot(0, 0), zpeer)

    def exchanged(self):
        self.w.recv(self.tag + "z")

    def start(self, other):
        for d in (1, 3) if self.relayed else (1, 3, 2):
            self.pass_on(f"{other}{d}", self.slot(0, other), self.ring(d))
        self.have(0, other)

    def arrive(self, other, d):
        self.w.recv(f"{self.tag}{other}{d}")
        if self.relayed and (other, d) in ((0, 1), (1, 3)):
            self.pass_on(f"{other}2", self.slot(4 - d, other), self.ring(d))
        self.have(4 - d, other)

    def rest(self):
        for d, other in self.shared:
            self.w.recv(f"{self.tag}core{d}{other}")
            self.done(self.slot(d, other) + 8 - 2 * self.base)


def row_gather(wire, stream, place, out, done, relayed):
    return Gather(
        wire, stream, "r", out, place.core * 8, place.x, place.zl, place.xpeer, place.sibling(), done, relayed
    )


def col_gather(wire, stream, place, out, done, relayed):
    return Gather(wire, stream, "c", out, 0, place.y, place.zh, place.ypeer, None, done, relayed)


PARTS = 2


def greet(devices):
    barrier = pltpu.get_barrier_semaphore()
    for device in devices:
        pl.semaphore_signal(barrier, inc=1, device_id=device, device_id_type=MESH)
    return barrier


def prep_kernel(
    counts_hbm, tiles_hbm, whiten, xc, xrt, xct, tiles, xr, counts, packed, landed, wsem, lsem, send_sem, recv_sem
):
    place = Place()
    block = place.mine // 2
    to_row, to_col = place.x * 2 + place.zl, 2 * place.row + place.core
    from_row, from_col = place.col // 2, (place.row % 2) * 8 + (place.row // 2) * 2 + place.core
    moves = jnp.logical_or(to_row != place.row, to_col != place.col)
    peers = [place.at(col=(place.col + d) % 16) for d in range(1, 16)]
    peers += [place.ypeer(d) for d in (1, 2, 3)] + [place.zhpeer()]
    barrier = greet(peers)

    @pl.when(moves)
    def _():
        for device in ((to_row, to_col), (from_row, from_col)):
            pl.semaphore_signal(barrier, inc=1, device_id=device, device_id_type=MESH)

    counted = pltpu.make_async_copy(counts_hbm, counts, wsem.at[0])
    tiled = pltpu.make_async_copy(tiles_hbm, tiles, wsem.at[1])
    counted.start()
    tiled.start()
    counted.wait()
    for b in range(8):
        packed[b] = counts[:, b * 512 : (b + 1) * 512].astype(jnp.int16)
    pl.semaphore_wait(barrier, len(peers) + 2 * moves.astype(jnp.int32))

    wire = Wire(send_sem, recv_sem)
    for d in range(1, 16):
        c = (place.col + d) % 16
        b = (c % 2) * 4 + (c // 2) % 4
        wire.send(f"a{d}", packed.at[b], landed.at[place.col], place.at(col=c))
    landed[place.col] = packed[block]
    wire.recv(*[f"a{d}" for d in range(1, 16)])
    logged = jnp.log(1.0 + landed[...].astype(jnp.int32).astype(F32)).reshape(256, 512)
    mean = jnp.mean(logged, axis=0, keepdims=True)
    centered = logged - mean
    variance = jnp.mean(centered * centered, axis=0, keepdims=True)
    standard = (centered * lax.rsqrt(variance + epsilon)).astype(BF16)
    whitened = jnp.dot(standard, whiten[...], preferred_element_type=F32).astype(BF16)
    pair = block * 2
    for j in range(4):
        xr[pair + j // 2, j % 2 * 256 : (j % 2 + 1) * 256] = whitened[:, j * 128 : (j + 1) * 128]

    def turn(source, target, part):
        def done(s):
            for t in range(2 // PARTS * part, 2 // PARTS * (part + 1)):
                target[s, t * 128 : (t + 1) * 128] = source[s, t * 256 : (t + 1) * 256].T

        return done

    streams = [Stream(p, PARTS) for p in range(PARTS)]
    rows = [row_gather(wire, t, place, xr, turn(xr, xrt, t.part), True) for t in streams]
    cols = [col_gather(wire, t, place, xc, turn(xc, xct, t.part), True) for t in streams]
    hop = pltpu.make_async_remote_copy(
        src_ref=xr.at[place.mine], dst_ref=xc.at[to_row], send_sem=lsem.at[0],
        recv_sem=lsem.at[1], device_id=(to_row, to_col), device_id_type=MESH,
    )

    @pl.when(moves)
    def _():
        hop.start()

    @pl.when(jnp.logical_not(moves))
    def _():
        xc[place.mine_col] = xr[place.mine]

    for row in rows:
        row.start(0)
        row.start(1)

    @pl.when(moves)
    def _():
        hop.wait_recv()

    for col in cols:
        col.exchange(place.zhpeer())
        col.start(0)
    for row in rows:
        row.arrive(0, 1)
        row.arrive(1, 3)
    for col in cols:
        col.arrive(0, 1)
        col.exchanged()
        col.start(1)
    for col in cols:
        col.arrive(0, 3)
    for other, d in ((0, 3), (1, 1), (0, 2), (1, 2)):
        for row in rows:
            row.arrive(other, d)
    for other, d in ((1, 3), (1, 1), (0, 2), (1, 2)):
        for col in cols:
            col.arrive(other, d)
    for row in rows:
        row.rest()
    tiled.wait()
    wire.drain()

    @pl.when(moves)
    def _():
        hop.wait_send()


def add(*parts):
    total = parts[0].astype(F32)
    for part in parts[1:]:
        total = total + part.astype(F32)
    return total


class Scatter:
    def __init__(self, wire, stream, tag, terms, slot, land, ztemp, keep, z, ring, zpeer):
        self.w, self.stream, self.tag = wire, stream, f"{tag}{stream.part}"
        self.terms, self.slot, self.land, self.ztemp, self.keep = terms, slot, land, ztemp, keep
        self.z, self.ring, self.zpeer = z, ring, zpeer

    def term(self, d, e):
        return self.stream.cut(self.terms, self.slot(d, e))

    def landed(self, i):
        return self.stream.cut(self.land, i)

    def put(self, name, i, src, device):
        self.w.send(self.tag + name, src, self.landed(i), device)

    def first(self):
        self.put("A1", 0, self.term(2, 0), self.ring(1))
        self.put("B1", 1, self.term(2, 1), self.ring(3))

    def second(self):
        self.put("A2", 2, self.term(1, 1), self.ring(1))
        self.put("B2", 3, self.term(3, 0), self.ring(3))

    def merge(self):
        for name, i, d, e, then in (("A1", 0, 1, 0, "A3"), ("B1", 1, 3, 1, "B3")):
            self.w.recv(self.tag + name)
            here = self.landed(i)
            here[...] = add(self.term(d, e)[...], here[...]).astype(BF16)
            self.put(then, 4 + i, here, self.ring(d))

    def cross(self):
        self.w.recv(*[self.tag + n for n in ("B2", "A2", "A3", "B3")])
        own = [
            add(self.term(0, e)[...], self.landed(i)[...], self.landed(j)[...]) for e, i, j in ((0, 3, 4), (1, 2, 5))
        ]
        mine = self.z == 0
        out = self.stream.cut(self.ztemp, 0)
        out[...] = jnp.where(mine, own[1], own[0]).astype(BF16)
        self.w.send(self.tag + "Z", out, self.stream.cut(self.ztemp, 1), self.zpeer)
        self.keep[self.stream.rows(self.keep)] = jnp.where(mine, own[0], own[1])

    def last(self, out, slot, turned):
        self.w.recv(self.tag + "Z")
        got = self.stream.cut(self.ztemp, 1)[...]
        total = add(self.keep[self.stream.rows(self.keep)], got).astype(BF16)
        self.stream.cut(out, slot)[...] = total.T if turned else total


class ZFirst:
    def __init__(self, wire, stream, place, summed, slot, zin, sums, xin, keep, out):
        self.w, self.stream, self.place, self.tag = wire, stream, place, f"zf{stream.part}"
        self.summed, self.slot, self.zin, self.sums, self.xin = summed, slot, zin, sums, xin
        self.keep, self.out, self.shared = keep, out, []

    def cross(self, d):
        src = self.stream.cut(self.summed, self.slot(d, 1 - self.place.zl))
        self.w.send(f"{self.tag}z{d}", src, self.stream.cut(self.zin, d), self.place.zlpeer())

    def merge(self, d):
        self.w.recv(f"{self.tag}z{d}")
        mine = self.stream.cut(self.summed, self.slot(d, self.place.zl))[...]
        total = add(mine, self.stream.cut(self.zin, d)[...])
        if d == 0:
            self.keep[self.stream.rows(self.keep)] = total
            return
        out = self.stream.cut(self.sums, d - 1)
        out[...] = total.astype(BF16)
        self.w.send(f"{self.tag}x{d}", out, self.stream.cut(self.xin, d - 1), self.place.xpeer(d))

    def last(self):
        parts = [self.keep[self.stream.rows(self.keep)]]
        for d in (1, 2, 3):
            self.w.recv(f"{self.tag}x{d}")
            parts.append(self.stream.cut(self.xin, d - 1)[...])
        self.stream.cut(self.out, self.place.mine)[...] = add(*parts).astype(BF16)
        for d in (1, 3, 2):
            self.pass_on(f"g{d}", self.at(0, 0), self.place.xpeer(d))
        self.pass_on("c0", self.at(0, 0), self.place.zlpeer())
        self.have(0, 0)

    def at(self, d, other):
        z = 1 - self.place.zl if other else self.place.zl
        return self.place.core * 8 + ((self.place.x + d) % 4) * 2 + z

    def pass_on(self, name, slot, device):
        part = self.stream.cut(self.out, slot)
        self.w.send(self.tag + name, part, part, device)

    def have(self, d, other):
        self.pass_on(f"core{d}{other}", self.at(d, other), self.place.sibling())
        self.shared.append((d, other))

    def near(self, d):
        self.w.recv(f"{self.tag}g{d}")
        self.pass_on(f"c{4 - d}", self.at(4 - d, 0), self.place.zlpeer())
        self.have(4 - d, 0)

    def beyond(self, d):
        self.w.recv(f"{self.tag}c{d}")
        self.have(d, 1)

    def rest(self):
        for d, other in self.shared:
            self.w.recv(f"{self.tag}core{d}{other}")


def reduce_kernel(rfull, cfull, u, v, rp, cp, pair, summed, rland, rtemp, rkeep, zin, sums, xin, cland, ctemp, ckeep, send_sem, recv_sem):
    place = Place()
    peers = [place.sibling(), place.zlpeer(), place.zhpeer()]
    peers += [place.xpeer(d) for d in (1, 2, 3)] + [place.ypeer(d) for d in (1, 2, 3)]
    barrier = greet(peers)
    rp[...] = rfull[...].astype(BF16)
    cp[...] = cfull[...].astype(BF16)
    pl.semaphore_wait(barrier, len(peers))
    wire = Wire(send_sem, recv_sem)
    here, there = place.core * 8, 8 - place.core * 8

    def rslot(d, e):
        return ((place.x + d) % 4) * 2 + e

    def cslot(d, e):
        return ((place.y + d) % 4) * 2 + e

    streams = [Stream(p, PARTS) for p in range(PARTS)]
    cols = [
        Scatter(wire, t, "cs", cp, cslot, cland, ctemp, ckeep, place.zh, place.ypeer, place.zhpeer()) for t in streams
    ]
    row = Scatter(wire, streams[0], "rs", summed, rslot, rland, rtemp, rkeep, place.zl, place.xpeer, place.zlpeer())
    other = ZFirst(wire, streams[1], place, summed, rslot, zin, sums, xin, rkeep, u)
    order = ((2, 0), (2, 1), (1, 1), (3, 0), (1, 0), (3, 1), (0, 0), (0, 1))
    for t in streams:
        for d, e in order:
            s = rslot(d, e)
            wire.send(f"s{t.part}{d}{e}", t.cut(rp, there + s), t.cut(pair, s), place.sibling())
    for col in cols:
        col.first()
        col.second()

    def join(t, which):
        for d, e in which:
            s = rslot(d, e)
            wire.recv(f"s{t.part}{d}{e}")
            t.cut(summed, s)[...] = add(t.cut(rp, here + s)[...], t.cut(pair, s)[...]).astype(BF16)

    one, two = streams
    join(one, order[:2])
    row.first()
    join(two, order[:2])
    other.cross(2)
    join(one, order[2:4])
    row.second()
    join(two, order[2:6])
    other.cross(1)
    other.cross(3)
    join(two, order[6:])
    other.cross(0)
    cols[0].merge()
    join(one, order[4:6])
    row.merge()
    other.merge(2)
    cols[1].merge()
    other.merge(1)
    other.merge(3)
    join(one, order[6:])
    cols[0].cross()
    row.cross()
    other.merge(0)
    cols[1].cross()
    nothing = lambda s: None
    rg = row_gather(wire, one, place, u, nothing, False)
    cgs = [col_gather(wire, t, place, v, nothing, False) for t in streams]
    for i in range(2):
        cols[i].last(v, place.mine_col, True)
        cgs[i].exchange(place.zhpeer())
        cgs[i].start(0)
        if i == 0:
            row.last(u, place.mine, False)
            rg.exchange(place.zlpeer())
            rg.start(0)
        else:
            other.last()
    for g in (cgs[0], rg):
        g.exchanged()
        g.start(1)
    for d in (1, 3, 2):
        cgs[0].arrive(0, d)
        rg.arrive(0, d)
    cgs[1].exchanged()
    cgs[1].start(1)
    for d in (1, 3, 2):
        other.near(d)
        cgs[1].arrive(0, d)
    other.beyond(0)
    for d in (1, 3, 2):
        cgs[0].arrive(1, d)
        rg.arrive(1, d)
    for d in (3, 1, 2):
        other.beyond(d)
        cgs[1].arrive(1, d)
    rg.rest()
    other.rest()
    wire.drain()


def live_groups(count):
    return (count[0] + GROUP - 1) // GROUP


def gradient(k, live, rows, cols, u, v, xrt, xc):
    sr, sc = rows[k], cols[k]
    left = jnp.dot(u[sr], xc[sc], preferred_element_type=F32)
    right = jnp.dot(xrt[sr], v[sc], preferred_element_type=F32)
    return jnp.where(k < live, (left + right) * (0.5 / 256), 0.0)


def shrunk(moved):
    t = step_size * penalty
    return moved - jnp.clip(moved, -t, t)


def fix_diagonal(g, live, rows, cols, where_at, grads, base, tiles, omega_out):
    for j in range(GROUP):
        k = g * GROUP + j

        @pl.when(jnp.logical_and(k < live, where_at[0] + rows[k] == where_at[1] + cols[k]))
        def _():
            moved = tiles[k] - step_size * grads[base + j]
            diagonal = 0.5 * (moved + jnp.sqrt(moved * moved + 4.0 * step_size))
            row = lax.broadcasted_iota(jnp.int32, (128, 128), 0)
            col = lax.broadcasted_iota(jnp.int32, (128, 128), 1)
            omega_out[k] = jnp.where(row == col, diagonal, omega_out[k])


def products(k, low, rows, cols, xrt, xct, rp, cp):
    sr, sc = rows[k], cols[k]
    rp[sr] += jnp.dot(low, xct[sc], preferred_element_type=F32)
    cp[sc] += jnp.dot(low.T, xrt[sr], preferred_element_type=F32)


def first_kernel(rows, cols, count, where_at, tiles, xrt, xct, rp, cp):
    rp[...] = jnp.zeros_like(rp)
    cp[...] = jnp.zeros_like(cp)
    live = count[0]

    def group(g, _):
        for j in range(GROUP):
            k = g * GROUP + j
            low = jnp.where(k < live, tiles[k], 0.0).astype(BF16)
            products(k, low, rows, cols, xrt, xct, rp, cp)
        return 0

    lax.fori_loop(0, live_groups(count), group, 0)


def middle_kernel(rows, cols, count, where_at, tiles, u, v, xrt, xc, xct, omega_out, rp, cp, grads):
    rp[...] = jnp.zeros_like(rp)
    cp[...] = jnp.zeros_like(cp)
    live = count[0]

    def group(g, _):
        for j in range(GROUP):
            k = g * GROUP + j
            grad = gradient(k, live, rows, cols, u, v, xrt, xc)
            grads[j] = grad
            omega_out[k] = shrunk(jnp.where(k < live, tiles[k], 0.0) - step_size * grad)
        fix_diagonal(g, live, rows, cols, where_at, grads, 0, tiles, omega_out)
        for j in range(GROUP):
            k = g * GROUP + j
            products(k, omega_out[k].astype(BF16), rows, cols, xrt, xct, rp, cp)
        return 0

    lax.fori_loop(0, live_groups(count), group, 0)


def last_kernel(rows, cols, count, where_at, tiles, u, v, xrt, xc, omega_out, grad_out, obuf, gbuf, zeros, sem):
    live = count[0]
    groups, total = live_groups(count), omega_out.shape[0] // GROUP

    def writes(g, o, d):
        here = pl.ds(g * GROUP, GROUP)
        return (
            pltpu.make_async_copy(o, omega_out.at[here], sem.at[0, g]),
            pltpu.make_async_copy(d, grad_out.at[here], sem.at[1, g]),
        )

    zeros[...] = jnp.zeros_like(zeros)

    def dead(g, _):
        for copy in writes(g, zeros, zeros):
            copy.start()
        return 0

    lax.fori_loop(groups, total, dead, 0)

    def group(g, _):
        for j in range(GROUP):
            k = g * GROUP + j
            grad = gradient(k, live, rows, cols, u, v, xrt, xc)
            gbuf[k] = grad
            obuf[k] = shrunk(jnp.where(k < live, tiles[k], 0.0) - step_size * grad)
        fix_diagonal(g, live, rows, cols, where_at, gbuf, g * GROUP, tiles, obuf)
        here = pl.ds(g * GROUP, GROUP)
        for copy in writes(g, obuf.at[here], gbuf.at[here]):
            copy.start()
        return 0

    lax.fori_loop(0, groups, group, 0)

    def wait(g, _):
        for copy in writes(g, zeros, zeros):
            copy.wait()
        return 0

    lax.fori_loop(0, total, wait, 0)


def tile_call(kernel, scalars, dense, out_shape, out_space, scratch, limit):
    smem = pl.BlockSpec(memory_space=pltpu.SMEM)
    vmem = pl.BlockSpec(memory_space=pltpu.VMEM)
    return pl.pallas_call(
        kernel,
        out_shape=out_shape,
        in_specs=[smem] * 4 + [vmem] * len(dense),
        out_specs=[pl.BlockSpec(memory_space=out_space)] * len(out_shape),
        scratch_shapes=scratch,
        compiler_params=pltpu.CompilerParams(vmem_limit_bytes=limit * MIB),
    )(*scalars, *dense)


def prep(counts, whiten, tiles):
    whiten = lax.dynamic_slice(whiten, (Place().mine // 2, 0, 0), (1, 512, 512)).reshape(512, 512)
    vmem = pl.BlockSpec(memory_space=pltpu.VMEM)
    n = 15 + PARTS * (14 + 7)
    shapes = ((8, 512, 128), (16, 256, 256), (8, 256, 256))
    return pl.pallas_call(
        prep_kernel,
        out_shape=[jax.ShapeDtypeStruct(s, BF16) for s in shapes] + [jax.ShapeDtypeStruct(tiles.shape, F32)],
        in_specs=[pl.BlockSpec(memory_space=pltpu.HBM)] * 2 + [vmem],
        out_specs=[vmem] * 4,
        scratch_shapes=[
            pltpu.VMEM((16, 512, 128), BF16),
            pltpu.VMEM((16, 4096), jnp.int32),
            pltpu.VMEM((8, 16, 512), jnp.int16),
            pltpu.VMEM((16, 16, 512), jnp.int16),
            pltpu.SemaphoreType.DMA((2,)),
            pltpu.SemaphoreType.DMA((2,)),
            pltpu.SemaphoreType.DMA((n,)),
            pltpu.SemaphoreType.DMA((n,)),
        ],
        compiler_params=pltpu.CompilerParams(collective_id=0, has_side_effects=True, vmem_limit_bytes=PREP_MIB * MIB),
    )(counts, tiles, whiten)


def reduce_both(rp, cp, collective_id):
    vmem = pl.BlockSpec(memory_space=pltpu.VMEM)
    n = PARTS * (8 + 7 + 7 + 15 + 7)
    u, v = pl.pallas_call(
        reduce_kernel,
        out_shape=[jax.ShapeDtypeStruct((16, 256, 256), BF16), jax.ShapeDtypeStruct((8, 512, 128), BF16)],
        in_specs=[vmem] * 2,
        out_specs=[vmem] * 2,
        scratch_shapes=[
            pltpu.VMEM((16, 256, 256), BF16),
            pltpu.VMEM((8, 256, 256), BF16),
            pltpu.VMEM((8, 256, 256), BF16),
            pltpu.VMEM((8, 256, 256), BF16),
            pltpu.VMEM((6, 256, 256), BF16),
            pltpu.VMEM((2, 256, 256), BF16),
            pltpu.VMEM((256, 256), F32),
            pltpu.VMEM((4, 256, 256), BF16),
            pltpu.VMEM((3, 256, 256), BF16),
            pltpu.VMEM((3, 256, 256), BF16),
            pltpu.VMEM((6, 256, 256), BF16),
            pltpu.VMEM((2, 256, 256), BF16),
            pltpu.VMEM((256, 256), F32),
            pltpu.SemaphoreType.DMA((n,)),
            pltpu.SemaphoreType.DMA((n,)),
        ],
        compiler_params=pltpu.CompilerParams(
            collective_id=collective_id, has_side_effects=True, vmem_limit_bytes=12 * MIB
        ),
    )(rp.reshape(16, 256, 256), cp.reshape(8, 256, 256))
    return u.reshape(32, 128, 256), v.reshape(16, 256, 128)


def local(counts, whiten, initial_tiles, tile_rows, tile_cols, tile_count):
    where_at = jnp.stack([lax.axis_index("row") * 32, lax.axis_index("col") * 16]).astype(jnp.int32)
    scalars = (tile_rows.reshape(96), tile_cols.reshape(96), tile_count.reshape(1), where_at)
    xc, xrt, xct, tiles = prep(counts, whiten, initial_tiles.reshape(96, 128, 128))
    xc = xc.reshape(16, 256, 128)
    xrt, xct = xrt.reshape(32, 128, 256), xct.reshape(16, 128, 256)
    omega_shape = jax.ShapeDtypeStruct(tiles.shape, F32)
    part_shapes = [jax.ShapeDtypeStruct((n, 128, 256), F32) for n in (32, 16)]
    rp, cp = tile_call(first_kernel, scalars, (tiles, xrt, xct), part_shapes, pltpu.VMEM, [], 10)
    u, v = reduce_both(rp, cp, 1)
    omega, rp, cp = tile_call(
        middle_kernel, scalars, (tiles, u, v, xrt, xc, xct), [omega_shape] + part_shapes, pltpu.VMEM,
        [pltpu.VMEM((GROUP, 128, 128), F32)], 10,
    )
    u, v = reduce_both(rp, cp, 2)
    buffers = [pltpu.VMEM(tiles.shape, F32)] * 2 + [pltpu.VMEM((GROUP, 128, 128), F32)]
    omega, grad = tile_call(
        last_kernel, scalars, (omega, u, v, xrt, xc), [omega_shape] * 2, pltpu.HBM,
        buffers + [pltpu.SemaphoreType.DMA((2, 96 // GROUP))], 20,
    )
    return omega.reshape(initial_tiles.shape), grad.reshape(initial_tiles.shape)


def solution(mesh):
    in_specs = (
        P("col", "row"),
        P("row", None, None),
        P("row", "col", None, None, None),
        P("row", "col", None),
        P("row", "col", None),
        P("row", "col"),
    )
    out_specs = (P("row", "col", None, None, None), P("row", "col", None, None, None))
    return jax.shard_map(local, mesh=mesh, in_specs=in_specs, out_specs=out_specs, check_vma=False)
```
